32 devices in a mesh: pipe: 4 (over y, x), tensor: 4 (over z), dp: 2 (over core).
Axes of the slice: x: 2, y: 2, z: 4, core: 2. Of those that a mesh axis runs over, the one named last changes fastest.
Arguments:
- hidden: bfloat16 [512, 5120], P('dp', ('pipe', 'tensor')), may hold values from -16 to 16
- head_weight: bfloat16 [18992, 5120], P(('pipe', 'tensor'), 'dp'), may hold values from -2 to 2
- labels: int32 [512], P('dp'), may hold values from 0 to 18991
- loss_weight: float32 [512], P('dp'), may hold values from 1 to 10
Outputs:
- hidden_grad: bfloat16 [512, 5120], P('dp', ('pipe', 'tensor'))
- head_grad: bfloat16 [18992, 5120], P(('pipe', 'tensor'), 'dp')
- token_loss: float32 [512], P('dp')
The draws below stay inside these ranges and needn't reach their ends.
All inputs are finite; a program needn't handle non-finite values.
Results may differ from the reference program's by a relative error of at most 0.0052.
Values may be sent and summed in bfloat16 or wider, within the bound.
A program may use at most 128 MiB of HBM per device.

```python
import math
import jax
import jax.numpy as jnp
from jax import lax

D = 5120
VOC_DEV = 1187
VOCAB = 18992
TOKENS = 512
N_PIPE = 4
N_TENSOR = 4


def row_keys(base_key, vocab_rows):
    return jax.vmap(lambda index: jax.random.fold_in(base_key, index))(vocab_rows)


def row_scale(base_key, vocab_rows):
    keys = row_keys(base_key, vocab_rows)
    spread = jax.vmap(lambda row_key: jax.random.uniform(jax.random.fold_in(row_key, 1), ()))(keys)
    rising = 1.0 + 2.0 * vocab_rows.astype(jnp.float32) / (VOCAB - 1)
    return jnp.exp(spread * math.log(10.0)) * rising


def shared_direction(base_key):
    common_key = jax.random.fold_in(base_key, 2)
    return jnp.clip(jax.random.normal(common_key, (D,)), -4.0, 4.0)


def normal_rows(base_key, vocab_rows):
    keys = row_keys(base_key, vocab_rows)
    return jax.vmap(lambda row_key: jnp.clip(jax.random.normal(row_key, (D,)), -5.0, 5.0))(keys)


def shaped_rows(base_key, vocab_rows, unit_rows):
    common = shared_direction(base_key)
    mixed = 0.6 * common[None, :] + 0.8 * unit_rows
    return mixed * (row_scale(base_key, vocab_rows) / math.sqrt(D))[:, None]


def draw_head_weight(key, part):
    key = jax.random.fold_in(key, 11)
    vocab_rows = jnp.arange(VOCAB, dtype=jnp.int32)
    unit_rows = normal_rows(key, vocab_rows)
    values = shaped_rows(key, vocab_rows, unit_rows)
    return jnp.clip(values, -2.0, 2.0).astype(jnp.bfloat16)


def draw_hidden(key, part):
    key = jax.random.fold_in(key, 23)
    scale_key = jax.random.fold_in(key, 0)
    values_key = jax.random.fold_in(key, 2)
    flat_key = jax.random.fold_in(key, 4)
    row_spread = 0.3 * jnp.exp(jax.random.uniform(scale_key, (TOKENS, 1)) * math.log(10.0))
    flat_rows = jax.random.uniform(flat_key, (TOKENS, 1)) < 0.12
    row_spread = jnp.where(flat_rows, 0.01, row_spread)
    values = row_spread * jnp.clip(jax.random.normal(values_key, (TOKENS, D)), -4.0, 4.0)
    return jnp.clip(values, -16.0, 16.0).astype(jnp.bfloat16)


def set_ends(values, stream_key, smallest, largest):
    index_at = [jax.random.randint(jax.random.fold_in(stream_key, axis), (), 0, length) for axis, length in enumerate(values.shape)]
    widest = values.shape.index(max(values.shape))
    next_to = index_at[:widest] + [(index_at[widest] + 1) % values.shape[widest]] + index_at[widest + 1:]
    return values.at[tuple(index_at)].set(smallest).at[tuple(next_to)].set(largest)


def levels(rng, shape, shards, least, top_value):
    gain = 1.0
    for position, shards_of in shards:
        steps = jax.random.uniform(jax.random.fold_in(jax.random.fold_in(rng, 6), position), (shards_of,), jnp.float32, least / len(shards), top_value / len(shards))
        gain = gain * jnp.repeat(jnp.exp(steps), shape[position] // shards_of).reshape((-1,) + (1,) * (len(shape) - 1 - position))
    return gain


def setup_inputs(seed: int = 0) -> dict:
    splits = jax.random.split(jax.random.key(seed), 5)
    return {
        "hidden": draw_hidden(jax.random.fold_in(splits[4], 71), 0),
        "head_weight": draw_head_weight(jax.random.fold_in(splits[4], 71), 0),
        "labels": set_ends(jax.random.randint(splits[2], (TOKENS,), 0, VOCAB), jax.random.fold_in(splits[2], 1), 0, VOCAB - 1).astype(jnp.int32),
        "loss_weight": jnp.clip(jnp.exp(math.log(10.0) - 2.3025851 * jax.random.uniform(splits[3], (TOKENS,), jnp.float32) ** levels(splits[3], (TOKENS,), ((0, 2),), -0.2, 0.2)), 1.0, 10.0),
    }


def reference(hidden, head_weight, labels, loss_weight):
    logits = lax.dot_general(hidden, head_weight, (((1,), (1,)), ((), ())), preferred_element_type=jnp.float32)
    row_peak = lax.optimization_barrier(jnp.max(logits, axis=1, keepdims=True))
    shifted_exp = jnp.exp(logits - row_peak)
    row_total = lax.optimization_barrier(jnp.sum(shifted_exp, axis=1, keepdims=True))
    vocab_rows = jnp.arange(logits.shape[1], dtype=jnp.int32)
    target_mask = (vocab_rows[None, :] == labels[:, None]).astype(jnp.float32)
    picked = lax.optimization_barrier(jnp.sum(target_mask * logits, axis=1))
    token_loss = row_peak[:, 0] + jnp.log(row_total[:, 0]) - picked
    logit_grad = (loss_weight[:, None] * (shifted_exp / row_total - target_mask)).astype(jnp.bfloat16)
    hidden_grad = jnp.dot(logit_grad, head_weight, preferred_element_type=jnp.float32).astype(jnp.bfloat16)
    blocks = logit_grad.T.reshape(N_PIPE * N_TENSOR, VOC_DEV, TOKENS)

    def block_grad(block):
        return jnp.dot(block, hidden, preferred_element_type=jnp.float32).astype(jnp.bfloat16)
    head_grad = lax.map(block_grad, blocks).reshape(VOCAB, D)
    return (hidden_grad, head_grad, token_loss)
```

```python
import functools

import jax
import jax.numpy as jnp
from jax import lax
from jax.experimental import pallas as pl
from jax.experimental.pallas import tpu as pltpu
from jax.sharding import PartitionSpec as P

GROUP = ("pipe", "tensor")
MESH = pl.DeviceIdType.MESH
VMEM = pl.BlockSpec(memory_space=pltpu.VMEM)
ANY = pl.BlockSpec(memory_space=pl.ANY)
VMEM_BYTES = 48 * 1024 * 1024
Z = 4


def spans(rows, size):
    return [(start, min(size, rows - start)) for start in range(0, rows, size)]


class Place:
    def __init__(self):
        pipe = lax.axis_index("pipe")
        self.pipe = pipe
        self.x, self.y = pipe % 2, pipe // 2
        self.z = lax.axis_index("tensor")
        self.core = lax.axis_index("dp")
        self.home = self.y == self.core
        self.away = self.y == 1 - self.core
        self.x_peer = {"pipe": self.y * 2 + 1 - self.x}
        self.y_peer = {"pipe": (1 - self.y) * 2 + self.x}
        self.up = {"tensor": self.z + 1}
        self.down = {"tensor": self.z - 1}
        self.mate = {"dp": 1 - self.core}


def remote(src, dst, send_sem, recv_sem, device):
    return pltpu.make_async_remote_copy(
        src_ref=src, dst_ref=dst, send_sem=send_sem, recv_sem=recv_sem, device_id=device, device_id_type=MESH
    )


def greet_group(me, n):
    barrier = pltpu.get_barrier_semaphore()
    index = me.pipe * Z + me.z

    def greet(step, carry):
        other = (index + step) % n
        pl.semaphore_signal(
            barrier, inc=1, device_id={"pipe": other // Z, "tensor": other % Z}, device_id_type=MESH
        )
        return carry

    lax.fori_loop(1, n, greet, 0)
    pl.semaphore_signal(barrier, inc=1, device_id=me.mate, device_id_type=MESH)
    pl.semaphore_wait(barrier, n)


def forward_kernel(
    n, block, piece, weight, labels, loss_weight,
    features_out, grad_out, loss_out,
    features, weight_here, partial, partial_in, grad_here, stats,
    recv, send_up, send_down, send_x, send_y, send_y2, own_sem, weight_sem,
    mate_sems, stat_send, stat_recv, out_sems,
):
    me = Place()
    tokens = piece.shape[1]
    rows = weight.shape[0]
    x, z, core = me.x, me.z, me.core
    load_weight = pltpu.make_async_copy(weight, weight_here, weight_sem)
    load_weight.start()
    greet_group(me, n)

    def at(ref, column, level, half):
        start = pl.multiple_of((column * Z + level) * block, block)
        return ref.at[pl.ds(start, block), pl.ds(pl.multiple_of(half * tokens, tokens), tokens)]

    def copy(column, level, half, send_sem, device):
        here = at(features, column, level, half)
        return remote(here, here, send_sem, recv.at[(column * Z + level) * 2 + half], device)

    def arrived(column, level, half):
        copy(column, level, half, send_y.at[0], me.mate).wait_recv()

    def line_sends(level, half, sign):
        slot = level * 2 + half
        if sign <= 0:
            pl.when(z < Z - 1)(lambda: run(copy(x, level, half, send_up.at[slot], me.up)))
        if sign >= 0:
            pl.when(z > 0)(lambda: run(copy(x, level, half, send_down.at[slot], me.down)))
        run(copy(x, level, half, send_x.at[slot], me.x_peer))
        run(copy(x, level, half, send_y.at[slot], me.y_peer))

    def run(transfer):
        if waiting:
            transfer.wait_send()
        else:
            transfer.start()

    def line_step(distance, sign):
        level = z + sign * distance

        def home():
            for half in (0, 1):
                if not waiting:
                    arrived(x, level, half)
                line_sends(level, half, sign)

        def away():
            if not waiting:
                arrived(x, level, 0)
            run(copy(x, level, 0, send_x.at[level * 2], me.x_peer))
            if not waiting:
                arrived(x, level, 1)

        valid = (level >= 0) & (level < Z)
        pl.when(valid & me.home)(home)
        pl.when(valid & me.away)(away)

    def first_step():
        @pl.when(me.home)
        def _():
            line_sends(z, core, 0)
            if not waiting:
                arrived(x, z, 1 - core)
            line_sends(z, 1 - core, 0)

        @pl.when(me.away)
        def _():
            if not waiting:
                arrived(x, z, 0)
            run(copy(x, z, 0, send_x.at[z * 2], me.x_peer))
            if not waiting:
                arrived(x, z, 1)

    def peer_step(distance, sign):
        level = z + sign * distance

        def home():
            if not waiting:
                arrived(1 - x, level, 0)
                arrived(1 - x, level, 1)
            run(copy(1 - x, level, 1, send_y2.at[level], me.y_peer))

        def away():
            arrived(1 - x, level, 0)
            arrived(1 - x, level, 1)

        valid = (level >= 0) & (level < Z)
        pl.when(valid & me.home)(home)
        if not waiting:
            pl.when(valid & me.away)(away)

    def multiply(pair, half, first):
        width = 2 * block
        depth = pl.ds(pl.multiple_of(pair * width, width), width)
        right = features[depth, pl.ds(pl.multiple_of(half * tokens, tokens), tokens)]
        for start, size in spans(rows, 592):
            part = jnp.dot(weight_here[pl.ds(start, size), depth], right, preferred_element_type=jnp.float32)
            where = (half, pl.ds(start, size))
            partial[where] = part if first else partial[where] + part

    def multiply_both(pair, first=False):
        def step(half, carry):
            multiply(pair, half, first)
            return carry

        lax.fori_loop(0, 2, step, 0)

    waiting = False
    own_copy = pltpu.make_async_copy(piece, at(features, x, z, core), own_sem)
    own_send = remote(
        piece, at(features, x, z, core), own_sem, recv.at[(x * Z + z) * 2 + core], me.mate
    )
    pl.when(me.home)(own_copy.start)
    pl.when(me.away)(own_send.start)
    pl.when(me.home)(own_copy.wait)
    first_step()
    for sign in (-1, 1):
        line_step(1, sign)
    peer_step(0, 1)
    load_weight.wait()
    multiply_both(x * 2 + z // 2, True)
    for sign in (-1, 1):
        line_step(2, sign)
    for sign in (-1, 1):
        peer_step(1, sign)
    for sign in (-1, 1):
        line_step(3, sign)
    for sign in (-1, 1):
        peer_step(2, sign)
    multiply_both(x * 2 + 1 - z // 2)
    multiply_both((1 - x) * 2 + z // 2)
    for sign in (-1, 1):
        peer_step(3, sign)
    store_features = pltpu.make_async_copy(features, features_out, out_sems.at[0])
    store_features.start()
    last = (1 - x) * 2 + 1 - z // 2
    multiply(last, 1 - core, False)
    swap = remote(partial.at[1 - core], partial_in, mate_sems.at[0], mate_sems.at[1], me.mate)
    swap.start()
    multiply(last, core, False)

    waiting = True
    pl.when(me.away)(own_send.wait_send)
    first_step()
    peer_step(0, 1)
    for distance in (1, 2, 3):
        for sign in (-1, 1):
            line_step(distance, sign)
            peer_step(distance, sign)
    swap.wait()

    index = me.pipe * Z + z
    target = labels[...] - index * rows
    peak = jnp.full((1, tokens), -jnp.inf, jnp.float32)
    picked = jnp.zeros((1, tokens), jnp.float32)
    parts = spans(rows, 128)

    def is_target(start, size):
        return lax.broadcasted_iota(jnp.int32, (size, tokens), 0) + start == target

    for start, size in parts:
        where = pl.ds(start, size)
        logits = partial[core, where] + partial_in[where]
        partial_in[where] = logits
        peak = jnp.maximum(peak, jnp.max(logits, axis=0, keepdims=True))
        picked += jnp.sum(jnp.where(is_target(start, size), logits, 0.0), axis=0, keepdims=True)
    total = jnp.zeros((1, tokens), jnp.float32)
    for start, size in parts:
        total += jnp.sum(jnp.exp(partial_in[pl.ds(start, size)] - peak), axis=0, keepdims=True)
    stats[index] = jnp.concatenate([peak, total, picked, jnp.zeros((5, tokens), jnp.float32)], axis=0)

    def stat_copy(step):
        other = (index + step) % n
        device = {"pipe": other // Z, "tensor": other % Z}
        return remote(stats.at[index], stats.at[index], stat_send.at[step], stat_recv.at[index], device)

    def send_stat(step, carry):
        stat_copy(step).start()
        return carry

    def wait_stat(step, carry):
        other = (index + step) % n
        remote(
            stats.at[other], stats.at[other], stat_send.at[step], stat_recv.at[other], me.mate
        ).wait_recv()
        return carry

    def wait_stat_send(step, carry):
        stat_copy(step).wait_send()
        return carry

    lax.fori_loop(1, n, send_stat, 0)
    lax.fori_loop(1, n, wait_stat, 0)
    every = stats[...]
    peaks, totals, picks = every[:, 0], every[:, 1], every[:, 2]
    row_peak = jnp.max(peaks, axis=0, keepdims=True)
    row_total = jnp.sum(totals * jnp.exp(peaks - row_peak), axis=0, keepdims=True)
    loss_out[...] = row_peak + jnp.log(row_total) - jnp.sum(picks, axis=0, keepdims=True)
    scale = loss_weight[...]
    inverse = 1.0 / row_total
    for start, size in parts:
        where = pl.ds(start, size)
        share = jnp.exp(partial_in[where] - row_peak) * inverse
        hit = jnp.where(is_target(start, size), 1.0, 0.0)
        grad_here[where] = (scale * (share - hit)).astype(jnp.bfloat16)
    mine = grad_out.at[:, pl.ds(pl.multiple_of(core * tokens, tokens), tokens)]
    keep = pltpu.make_async_copy(grad_here, mine, out_sems.at[1])
    share_grad = remote(grad_here, mine, mate_sems.at[2], mate_sems.at[3], me.mate)
    share_grad.start()
    keep.start()
    lax.fori_loop(1, n, wait_stat_send, 0)
    keep.wait()
    share_grad.wait()
    store_features.wait()


def forward(hidden_t, head_weight, labels, loss_weight, n):
    block, tokens = hidden_t.shape
    rows, width = head_weight.shape
    dma = pltpu.SemaphoreType.DMA
    return pl.pallas_call(
        functools.partial(forward_kernel, n, block),
        out_shape=(
            jax.ShapeDtypeStruct((width, 2 * tokens), jnp.bfloat16),
            jax.ShapeDtypeStruct((rows, 2 * tokens), jnp.bfloat16),
            jax.ShapeDtypeStruct((1, tokens), jnp.float32),
        ),
        in_specs=[VMEM, ANY, VMEM, VMEM],
        out_specs=(ANY, ANY, VMEM),
        scratch_shapes=[
            pltpu.VMEM((width, 2 * tokens), jnp.bfloat16),
            pltpu.VMEM((rows, width), jnp.bfloat16),
            pltpu.VMEM((2, rows, tokens), jnp.float32),
            pltpu.VMEM((rows, tokens), jnp.float32),
            pltpu.VMEM((rows, tokens), jnp.bfloat16),
            pltpu.VMEM((n, 8, tokens), jnp.float32),
            dma((16,)), dma((8,)), dma((8,)), dma((8,)), dma((8,)), dma((4,)), dma, dma,
            dma((4,)), dma((n,)), dma((n,)), dma((2,)),
        ],
        compiler_params=pltpu.CompilerParams(
            collective_id=0, has_side_effects=True, vmem_limit_bytes=VMEM_BYTES
        ),
    )(hidden_t, head_weight, labels, loss_weight)


def reduce_kernel(
    block, term, out,
    from_y, from_x, from_below, from_above, passed, summed, final, landed,
    recv_y, recv_x, recv_below, recv_above, recv_final,
    send_x, send_pass, send_y, send_z, send_final,
):
    me = Place()
    tokens = out.shape[1]
    x, z, core = me.x, me.z, me.core
    barrier = pltpu.get_barrier_semaphore()
    for peer in (me.x_peer, me.y_peer, me.mate):
        pl.semaphore_signal(barrier, inc=1, device_id=peer, device_id_type=MESH)

    @pl.when(z > 0)
    def _():
        pl.semaphore_signal(barrier, inc=1, device_id=me.down, device_id_type=MESH)

    @pl.when(z < Z - 1)
    def _():
        pl.semaphore_signal(barrier, inc=1, device_id=me.up, device_id_type=MESH)

    pl.semaphore_wait(barrier, 3 + (z + Z - 1) // Z + (2 * (Z - 1) - z) // Z)

    def own(column, level, half):
        start = pl.multiple_of((column * Z + level) * block, block)
        return term.at[pl.ds(start, block), pl.ds(pl.multiple_of(half * tokens, tokens), tokens)]

    upper = z // 2
    order = (3 * (1 - upper), 2 - upper, 1 - z + 4 * upper, z)

    def away_cross(level):
        return remote(own(1 - x, level, 0), from_x.at[level * 2], send_x.at[level], recv_x.at[level * 2], me.x_peer)

    def away_diagonal(level):
        return remote(own(1 - x, level, 1), from_y.at[8 + level], send_y.at[8 + level], recv_y.at[8 + level], me.y_peer)

    def away_line(level, half):
        slot = level * 2 + half
        source = own(x, level, 1) if half else passed.at[level]
        return remote(source, from_y.at[slot], send_y.at[slot], recv_y.at[slot], me.y_peer)

    def home_cross(level, half):
        slot = level * 2 + half
        source = passed.at[level] if half else own(1 - x, level, 0)
        sem = send_pass.at[level] if half else send_x.at[level]
        return remote(source, from_x.at[slot], sem, recv_x.at[slot], me.x_peer)

    def rise(level, half):
        slot = level * 2 + half
        return remote(summed.at[slot], from_below.at[slot], send_z.at[slot], recv_below.at[slot], me.up)

    def sink(level, half):
        slot = level * 2 + half
        return remote(summed.at[slot], from_above.at[slot], send_z.at[slot], recv_above.at[slot], me.down)

    def hand_over():
        return remote(final, landed, send_final, recv_final, me.mate)

    def f32(ref):
        return ref[...].astype(jnp.float32)

    @pl.when(me.away)
    def _():
        for level in order:
            away_cross(level).start()
            away_diagonal(level).start()
            away_line(level, 1).start()
        for level in order:
            away_cross(level).wait_recv()
            passed[level] = (f32(own(x, level, 0)) + f32(from_x.at[level * 2])).astype(jnp.bfloat16)
            away_line(level, 0).start()
        for level in order:
            away_cross(level).wait_send()
            away_diagonal(level).wait_send()
            away_line(level, 1).wait_send()
            away_line(level, 0).wait_send()
        hand_over().wait_recv()
        out[...] = landed[...]

    @pl.when(me.home)
    def _():
        def pass_on(level):
            away_diagonal(level).wait_recv()
            passed[level] = (f32(own(1 - x, level, 1)) + f32(from_y.at[8 + level])).astype(jnp.bfloat16)
            home_cross(level, 1).start()

        def gather(level, half):
            slot = level * 2 + half
            for inbox, sems in ((from_y, recv_y), (from_x, recv_x)):
                remote(final, inbox.at[slot], send_final, sems.at[slot], me.mate).wait_recv()
            return f32(own(x, level, half)) + f32(from_y.at[slot]) + f32(from_x.at[slot])

        def send_on(level):
            for half in (1, 0):
                slot = level * 2 + half
                total = gather(level, half)
                summed[slot] = total.astype(jnp.bfloat16)

                @pl.when((level < z) & (z < Z - 1))
                def _():
                    sink(level, half).wait_recv()
                    summed[slot] = (total + f32(from_above.at[slot])).astype(jnp.bfloat16)

                @pl.when((level > z) & (z > 0))
                def _():
                    rise(level, half).wait_recv()
                    summed[slot] = (total + f32(from_below.at[slot])).astype(jnp.bfloat16)

                pl.when(level < z)(lambda: sink(level, half).start())
                pl.when(level > z)(lambda: rise(level, half).start())

        for level in order:
            home_cross(level, 0).start()
        pass_on(order[0])
        pass_on(order[1])
        send_on(order[0])
        pass_on(order[2])
        send_on(order[1])
        pass_on(order[3])
        send_on(order[2])

        def finish(half, ref):
            slot = z * 2 + half
            total = gather(z, half)

            @pl.when(z == 0)
            def _():
                sink(z, half).wait_recv()
                ref[...] = (total + f32(from_above.at[slot])).astype(jnp.bfloat16)

            @pl.when(z == Z - 1)
            def _():
                rise(z, half).wait_recv()
                ref[...] = (total + f32(from_below.at[slot])).astype(jnp.bfloat16)

            @pl.when((z > 0) & (z < Z - 1))
            def _():
                sink(z, half).wait_recv()
                rise(z, half).wait_recv()
                ref[...] = (total + f32(from_above.at[slot]) + f32(from_below.at[slot])).astype(jnp.bfloat16)

        finish(1 - core, final)
        hand_over().start()
        finish(core, out)
        for level in order:
            for half in (0, 1):
                home_cross(level, half).wait_send()
                pl.when(level < z)(lambda: sink(level, half).wait_send())
                pl.when(level > z)(lambda: rise(level, half).wait_send())
        hand_over().wait_send()


def reduce_rows(term, block, tokens):
    dma = pltpu.SemaphoreType.DMA

    def pieces(count):
        return pltpu.VMEM((count, block, tokens), jnp.bfloat16)

    one = pltpu.VMEM((block, tokens), jnp.bfloat16)
    return pl.pallas_call(
        functools.partial(reduce_kernel, block),
        out_shape=jax.ShapeDtypeStruct((block, tokens), jnp.bfloat16),
        in_specs=[VMEM],
        out_specs=VMEM,
        scratch_shapes=[
            pieces(12), pieces(8), pieces(8), pieces(8), pieces(4), pieces(8), one, one,
            dma((12,)), dma((8,)), dma((8,)), dma((8,)), dma,
            dma((4,)), dma((4,)), dma((12,)), dma((8,)), dma,
        ],
        compiler_params=pltpu.CompilerParams(
            collective_id=1, has_side_effects=True, vmem_limit_bytes=VMEM_BYTES
        ),
    )(term)


def per_device_chips(n, hidden, head_weight, labels, loss_weight):
    tokens, block = hidden.shape
    features, logit_grad, token_loss = forward(
        hidden.T, head_weight, labels.reshape(1, tokens), loss_weight.reshape(1, tokens), n
    )
    term = lax.dot_general(
        head_weight, logit_grad, (((0,), (0,)), ((), ())), preferred_element_type=jnp.float32
    ).astype(jnp.bfloat16)
    hidden_grad = reduce_rows(term, block, tokens).T
    head_grad = lax.dot_general(
        logit_grad, features, (((1,), (1,)), ((), ())), preferred_element_type=jnp.float32
    ).astype(jnp.bfloat16)
    return hidden_grad, head_grad, token_loss.reshape(tokens)


def per_device(hidden, head_weight, labels, loss_weight):
    tokens = hidden.shape[0]
    rows = head_weight.shape[0]
    features = lax.all_gather(hidden, GROUP, axis=1, tiled=True)
    features = lax.all_to_all(features, "dp", split_axis=1, concat_axis=0, tiled=True)
    partial = lax.dot_general(
        head_weight, features, (((1,), (1,)), ((), ())), preferred_element_type=jnp.float32
    )
    logits = lax.psum_scatter(partial, "dp", scatter_dimension=1, tiled=True)
    entries = lax.axis_index(GROUP) * rows + jnp.arange(rows, dtype=jnp.int32)
    mask = (entries[:, None] == labels[None, :]).astype(jnp.float32)
    row_peak = lax.pmax(jnp.max(logits, axis=0), GROUP)
    shifted_exp = jnp.exp(logits - row_peak[None, :])
    row_total, picked = lax.psum((jnp.sum(shifted_exp, axis=0), jnp.sum(mask * logits, axis=0)), GROUP)
    token_loss = row_peak + jnp.log(row_total) - picked
    grad = (loss_weight[None, :] * (shifted_exp / row_total[None, :] - mask)).astype(jnp.bfloat16)
    grad = lax.all_gather(grad, "dp", axis=1, tiled=True)
    head_grad = jnp.dot(grad, features, preferred_element_type=jnp.float32).astype(jnp.bfloat16)
    term = lax.dot_general(grad, head_weight, (((0,), (0,)), ((), ())), preferred_element_type=jnp.float32)
    term = lax.all_to_all(term, "dp", split_axis=0, concat_axis=1, tiled=True)
    hidden_grad = lax.psum_scatter(term, GROUP, scatter_dimension=1, tiled=True).astype(jnp.bfloat16)
    return hidden_grad, head_grad, token_loss


def solution(mesh):
    sizes = dict(mesh.shape)
    if (sizes["pipe"], sizes["tensor"], sizes["dp"]) == (4, Z, 2):
        body = functools.partial(per_device_chips, 4 * Z)
    else:
        body = per_device
    return jax.shard_map(
        body,
        mesh=mesh,
        in_specs=(P("dp", GROUP), P(GROUP, "dp"), P("dp"), P("dp")),
        out_specs=(P("dp", GROUP), P(GROUP, "dp"), P("dp")),
        check_vma=False,
    )
```

```python
import functools

import jax
import jax.numpy as jnp
from jax import lax
from jax.experimental import pallas as pl
from jax.experimental.pallas import tpu as pltpu
from jax.sharding import PartitionSpec as P

GROUP = ("pipe", "tensor")
MESH = pl.DeviceIdType.MESH
VMEM = pl.BlockSpec(memory_space=pltpu.VMEM)
ANY = pl.BlockSpec(memory_space=pl.ANY)
VMEM_BYTES = 48 * 1024 * 1024
Z = 4


def spans(rows, size):
    return [(start, min(size, rows - start)) for start in range(0, rows, size)]


class Place:
    def __init__(self):
        pipe = lax.axis_index("pipe")
        self.pipe = pipe
        self.x, self.y = pipe % 2, pipe // 2
        self.z = lax.axis_index("tensor")
        self.core = lax.axis_index("dp")
        self.home = self.y == self.core
        self.away = self.y == 1 - self.core
        self.x_peer = {"pipe": self.y * 2 + 1 - self.x}
        self.y_peer = {"pipe": (1 - self.y) * 2 + self.x}
        self.up = {"tensor": self.z + 1}
        self.down = {"tensor": self.z - 1}
        self.mate = {"dp": 1 - self.core}


def remote(src, dst, send_sem, recv_sem, device):
    return pltpu.make_async_remote_copy(
        src_ref=src, dst_ref=dst, send_sem=send_sem, recv_sem=recv_sem, device_id=device, device_id_type=MESH
    )


def greet_group(me, n):
    barrier = pltpu.get_barrier_semaphore()
    index = me.pipe * Z + me.z

    def greet(step, carry):
        other = (index + step) % n
        pl.semaphore_signal(
            barrier, inc=1, device_id={"pipe": other // Z, "tensor": other % Z}, device_id_type=MESH
        )
        return carry

    lax.fori_loop(1, n, greet, 0)
    pl.semaphore_signal(barrier, inc=1, device_id=me.mate, device_id_type=MESH)
    pl.semaphore_wait(barrier, n)


def forward_kernel(
    n, block, piece, weight, labels_in, loss_weight_in,
    features_out, grad_out, loss_out,
    features, weight_here, partial, partial_in, grad_here, stats, labels, loss_weight,
    recv, recv_low, send_up, send_down, low_up, low_down, send_x, send_y, send_y2, own_sem, weight_sem,
    mate_sems, stat_send, stat_recv, out_sems, token_sems,
):
    me = Place()
    tokens = piece.shape[1]
    rows = weight.shape[0]
    x, z, core = me.x, me.z, me.core
    load_weight = pltpu.make_async_copy(weight, weight_here, weight_sem)
    load_weight.start()
    load_tokens = [
        pltpu.make_async_copy(labels_in, labels, token_sems.at[0]),
        pltpu.make_async_copy(loss_weight_in, loss_weight, token_sems.at[1]),
    ]
    for load in load_tokens:
        load.start()
    greet_group(me, n)
    low = block // 80 * 16
    whole, upper, lower = (0, block), (low, block - low), (0, low)

    def at(column, level, half, part):
        start = pl.multiple_of((column * Z + level) * block + part[0], 16)
        return features.at[pl.ds(start, part[1]), pl.ds(pl.multiple_of(half * tokens, tokens), tokens)]

    def copy(column, level, half, send_sem, device, part):
        here = at(column, level, half, part)
        sems = recv_low if part is lower else recv
        return remote(here, here, send_sem, sems.at[(column * Z + level) * 2 + half], device)

    def arrived(column, level, half, part):
        copy(column, level, half, send_y.at[0], me.mate, part).wait_recv()

    def run(transfer):
        if waiting:
            transfer.wait_send()
        else:
            transfer.start()

    def need(column, level, half, part):
        if not waiting:
            arrived(column, level, half, part)

    def line_sends(level, half, sign, part):
        slot = level * 2 + half
        if sign <= 0:
            pl.when(z < Z - 1)(lambda: run(copy(x, level, half, send_up.at[slot], me.up, upper)))
        if sign >= 0:
            pl.when(z > 0)(lambda: run(copy(x, level, half, send_down.at[slot], me.down, upper)))
        run(copy(x, level, half, send_x.at[slot], me.x_peer, part))
        run(copy(x, level, half, send_y.at[slot], me.y_peer, part))

    def line_step(distance, sign):
        level = z + sign * distance

        def home():
            for half in (0, 1):
                need(x, level, half, upper)
                line_sends(level, half, sign, upper)

        def away():
            need(x, level, 0, upper)
            run(copy(x, level, 0, send_x.at[level * 2], me.x_peer, upper))
            need(x, level, 1, upper)

        valid = (level >= 0) & (level < Z)
        pl.when(valid & me.home)(home)
        pl.when(valid & me.away)(away)

    def first_step():
        @pl.when(me.home)
        def _():
            line_sends(z, core, 0, whole)
            need(x, z, 1 - core, whole)
            line_sends(z, 1 - core, 0, whole)

        @pl.when(me.away)
        def _():
            need(x, z, 0, whole)
            run(copy(x, z, 0, send_x.at[z * 2], me.x_peer, whole))
            need(x, z, 1, whole)

    def peer_step(distance, sign):
        level = z + sign * distance
        part = upper if distance else whole
        valid = (level >= 0) & (level < Z)
        if not waiting:
            @pl.when(valid)
            def _():
                arrived(1 - x, level, 0, part)
                arrived(1 - x, level, 1, part)

        pl.when(valid & me.home)(
            lambda: run(copy(1 - x, level, 1, send_y2.at[level], me.y_peer, part))
        )

    def low_step(distance, sign):
        level = z + sign * distance

        def each(which, carry):
            column, half = which // 2, which % 2
            slot = (column * Z + level) * 2 + half
            if distance:
                need(column, level, half, lower)
            if sign <= 0:
                pl.when(z < Z - 1)(lambda: run(copy(column, level, half, low_up.at[slot], me.up, lower)))
            if sign >= 0:
                pl.when(z > 0)(lambda: run(copy(column, level, half, low_down.at[slot], me.down, lower)))
            return carry

        @pl.when((level >= 0) & (level < Z))
        def _():
            lax.fori_loop(0, 4, each, 0)

    def multiply(pair, half, first):
        width = 2 * block
        depth = pl.ds(pl.multiple_of(pair * width, width), width)
        right = features[depth, pl.ds(pl.multiple_of(half * tokens, tokens), tokens)]
        for start, size in spans(rows, 592):
            part = jnp.dot(weight_here[pl.ds(start, size), depth], right, preferred_element_type=jnp.float32)
            where = (half, pl.ds(start, size))
            partial[where] = part if first else partial[where] + part

    def multiply_both(pair, first=False):
        def step(half, carry):
            multiply(pair, half, first)
            return carry

        lax.fori_loop(0, 2, step, 0)

    waiting = False
    mine = at(x, z, core, whole)
    own_copy = pltpu.make_async_copy(piece, mine, own_sem)
    own_send = remote(piece, mine, own_sem, recv.at[(x * Z + z) * 2 + core], me.mate)
    pl.when(me.home)(own_copy.start)
    pl.when(me.away)(own_send.start)
    pl.when(me.home)(own_copy.wait)
    first_step()
    for sign in (-1, 1):
        line_step(1, sign)
    peer_step(0, 1)
    low_step(0, 0)
    for sign in (-1, 1):
        line_step(2, sign)
    for sign in (-1, 1):
        peer_step(1, sign)
    for sign in (-1, 1):
        low_step(1, sign)
    load_weight.wait()
    multiply_both(x * 2 + z // 2, True)
    for sign in (-1, 1):
        line_step(3, sign)
    for sign in (-1, 1):
        peer_step(2, sign)
    for sign in (-1, 1):
        low_step(2, sign)
    multiply_both((1 - x) * 2 + z // 2)
    for sign in (-1, 1):
        peer_step(3, sign)
    for sign in (-1, 1):
        low_step(3, sign)
    store_features = pltpu.make_async_copy(features, features_out, out_sems.at[0])
    store_features.start()
    near, far = x * 2 + 1 - z // 2, (1 - x) * 2 + 1 - z // 2
    multiply(near, 1 - core, False)
    multiply(far, 1 - core, False)
    swap = remote(partial.at[1 - core], partial_in, mate_sems.at[0], mate_sems.at[1], me.mate)
    swap.start()
    multiply(near, core, False)
    multiply(far, core, False)

    waiting = True
    pl.when(me.away)(own_send.wait_send)
    first_step()
    peer_step(0, 1)
    low_step(0, 0)
    for distance in (1, 2, 3):
        for sign in (-1, 1):
            line_step(distance, sign)
            peer_step(distance, sign)
            low_step(distance, sign)
    for load in load_tokens:
        load.wait()
    swap.wait()

    index = me.pipe * Z + z
    target = labels[...] - index * rows
    peak = jnp.full((1, tokens), -jnp.inf, jnp.float32)
    picked = jnp.zeros((1, tokens), jnp.float32)
    parts = spans(rows, 128)

    def is_target(start, size):
        return lax.broadcasted_iota(jnp.int32, (size, tokens), 0) + start == target

    for start, size in parts:
        where = pl.ds(start, size)
        logits = partial[core, where] + partial_in[where]
        partial_in[where] = logits
        peak = jnp.maximum(peak, jnp.max(logits, axis=0, keepdims=True))
        picked += jnp.sum(jnp.where(is_target(start, size), logits, 0.0), axis=0, keepdims=True)
    total = jnp.zeros((1, tokens), jnp.float32)
    for start, size in parts:
        total += jnp.sum(jnp.exp(partial_in[pl.ds(start, size)] - peak), axis=0, keepdims=True)
    stats[index] = jnp.concatenate([peak, total, picked, jnp.zeros((5, tokens), jnp.float32)], axis=0)

    def stat_copy(step):
        other = (index + step) % n
        device = {"pipe": other // Z, "tensor": other % Z}
        return remote(stats.at[index], stats.at[index], stat_send.at[step], stat_recv.at[index], device)

    def send_stat(step, carry):
        stat_copy(step).start()
        return carry

    def wait_stat(step, carry):
        other = (index + step) % n
        remote(
            stats.at[other], stats.at[other], stat_send.at[step], stat_recv.at[other], me.mate
        ).wait_recv()
        return carry

    def wait_stat_send(step, carry):
        stat_copy(step).wait_send()
        return carry

    lax.fori_loop(1, n, send_stat, 0)
    lax.fori_loop(1, n, wait_stat, 0)
    every = stats[...]
    peaks, totals, picks = every[:, 0], every[:, 1], every[:, 2]
    row_peak = jnp.max(peaks, axis=0, keepdims=True)
    row_total = jnp.sum(totals * jnp.exp(peaks - row_peak), axis=0, keepdims=True)
    loss_out[...] = row_peak + jnp.log(row_total) - jnp.sum(picks, axis=0, keepdims=True)
    scale = loss_weight[...]
    inverse = 1.0 / row_total
    for start, size in parts:
        where = pl.ds(start, size)
        share = jnp.exp(partial_in[where] - row_peak) * inverse
        hit = jnp.where(is_target(start, size), 1.0, 0.0)
        grad_here[where] = (scale * (share - hit)).astype(jnp.bfloat16)
    mine = grad_out.at[:, pl.ds(pl.multiple_of(core * tokens, tokens), tokens)]
    keep = pltpu.make_async_copy(grad_here, mine, out_sems.at[1])
    share_grad = remote(grad_here, mine, mate_sems.at[2], mate_sems.at[3], me.mate)
    share_grad.start()
    keep.start()
    lax.fori_loop(1, n, wait_stat_send, 0)
    keep.wait()
    share_grad.wait()
    store_features.wait()


def forward(hidden_t, head_weight, labels, loss_weight, n):
    block, tokens = hidden_t.shape
    rows, width = head_weight.shape
    dma = pltpu.SemaphoreType.DMA
    return pl.pallas_call(
        functools.partial(forward_kernel, n, block),
        out_shape=(
            jax.ShapeDtypeStruct((width, 2 * tokens), jnp.bfloat16),
            jax.ShapeDtypeStruct((rows, 2 * tokens), jnp.bfloat16),
            jax.ShapeDtypeStruct((1, tokens), jnp.float32),
        ),
        in_specs=[ANY, ANY, ANY, ANY],
        out_specs=(ANY, ANY, VMEM),
        scratch_shapes=[
            pltpu.VMEM((width, 2 * tokens), jnp.bfloat16),
            pltpu.VMEM((rows, width), jnp.bfloat16),
            pltpu.VMEM((2, rows, tokens), jnp.float32),
            pltpu.VMEM((rows, tokens), jnp.float32),
            pltpu.VMEM((rows, tokens), jnp.bfloat16),
            pltpu.VMEM((n, 8, tokens), jnp.float32),
            pltpu.VMEM((1, tokens), jnp.int32),
            pltpu.VMEM((1, tokens), jnp.float32),
            dma((16,)), dma((16,)), dma((8,)), dma((8,)), dma((16,)), dma((16,)), dma((8,)), dma((8,)), dma((4,)),
            dma, dma, dma((4,)), dma((n,)), dma((n,)), dma((2,)), dma((2,)),
        ],
        compiler_params=pltpu.CompilerParams(
            collective_id=0, has_side_effects=True, vmem_limit_bytes=VMEM_BYTES
        ),
    )(hidden_t, head_weight, labels, loss_weight)


def reduce_kernel(
    block, term, out,
    from_y, from_x, from_below, from_above, passed, summed, final, landed,
    recv_y, recv_x, recv_below, recv_above, recv_final,
    send_x, send_pass, send_y, send_z, send_final,
):
    me = Place()
    tokens = out.shape[1]
    x, z, core = me.x, me.z, me.core
    barrier = pltpu.get_barrier_semaphore()
    for peer in (me.x_peer, me.y_peer, me.mate):
        pl.semaphore_signal(barrier, inc=1, device_id=peer, device_id_type=MESH)

    @pl.when(z > 0)
    def _():
        pl.semaphore_signal(barrier, inc=1, device_id=me.down, device_id_type=MESH)

    @pl.when(z < Z - 1)
    def _():
        pl.semaphore_signal(barrier, inc=1, device_id=me.up, device_id_type=MESH)

    pl.semaphore_wait(barrier, 3 + (z + Z - 1) // Z + (2 * (Z - 1) - z) // Z)

    def own(column, level, half):
        start = pl.multiple_of((column * Z + level) * block, block)
        return term.at[pl.ds(start, block), pl.ds(pl.multiple_of(half * tokens, tokens), tokens)]

    upper = z // 2
    order = (3 * (1 - upper), 2 - upper, 1 - z + 4 * upper, z)

    def away_cross(level):
        return remote(own(1 - x, level, 0), from_x.at[level * 2], send_x.at[level], recv_x.at[level * 2], me.x_peer)

    def away_diagonal(level):
        return remote(own(1 - x, level, 1), from_y.at[8 + level], send_y.at[8 + level], recv_y.at[8 + level], me.y_peer)

    def away_line(level, half):
        slot = level * 2 + half
        source = own(x, level, 1) if half else passed.at[level]
        return remote(source, from_y.at[slot], send_y.at[slot], recv_y.at[slot], me.y_peer)

    def home_cross(level, half):
        slot = level * 2 + half
        source = passed.at[level] if half else own(1 - x, level, 0)
        sem = send_pass.at[level] if half else send_x.at[level]
        return remote(source, from_x.at[slot], sem, recv_x.at[slot], me.x_peer)

    def rise(level, half):
        slot = level * 2 + half
        return remote(summed.at[slot], from_below.at[slot], send_z.at[slot], recv_below.at[slot], me.up)

    def sink(level, half):
        slot = level * 2 + half
        return remote(summed.at[slot], from_above.at[slot], send_z.at[slot], recv_above.at[slot], me.down)

    def hand_over():
        return remote(final, landed, send_final, recv_final, me.mate)

    def f32(ref):
        return ref[...].astype(jnp.float32)

    @pl.when(me.away)
    def _():
        away_cross(order[0]).start()
        away_diagonal(order[0]).start()
        for at, level in enumerate(order):
            away_line(level, 1).start()
            if at + 1 < Z:
                away_cross(order[at + 1]).start()
                away_diagonal(order[at + 1]).start()
            away_cross(level).wait_recv()
            passed[level] = (f32(own(x, level, 0)) + f32(from_x.at[level * 2])).astype(jnp.bfloat16)
            away_line(level, 0).start()
        for level in order:
            away_cross(level).wait_send()
            away_diagonal(level).wait_send()
            away_line(level, 1).wait_send()
            away_line(level, 0).wait_send()
        hand_over().wait_recv()
        out[...] = landed[...]

    @pl.when(me.home)
    def _():
        def pass_on(level):
            away_diagonal(level).wait_recv()
            passed[level] = (f32(own(1 - x, level, 1)) + f32(from_y.at[8 + level])).astype(jnp.bfloat16)
            home_cross(level, 1).start()

        def gather(level, half):
            slot = level * 2 + half
            for inbox, sems in ((from_y, recv_y), (from_x, recv_x)):
                remote(final, inbox.at[slot], send_final, sems.at[slot], me.mate).wait_recv()
            return f32(own(x, level, half)) + f32(from_y.at[slot]) + f32(from_x.at[slot])

        def send_on(level):
            for half in (1, 0):
                slot = level * 2 + half
                total = gather(level, half)
                summed[slot] = total.astype(jnp.bfloat16)

                @pl.when((level < z) & (z < Z - 1))
                def _():
                    sink(level, half).wait_recv()
                    summed[slot] = (total + f32(from_above.at[slot])).astype(jnp.bfloat16)

                @pl.when((level > z) & (z > 0))
                def _():
                    rise(level, half).wait_recv()
                    summed[slot] = (total + f32(from_below.at[slot])).astype(jnp.bfloat16)

                pl.when(level < z)(lambda: sink(level, half).start())
                pl.when(level > z)(lambda: rise(level, half).start())

        home_cross(order[0], 0).start()
        home_cross(order[1], 0).start()
        pass_on(order[0])
        home_cross(order[2], 0).start()
        pass_on(order[1])
        send_on(order[0])
        home_cross(order[3], 0).start()
        pass_on(order[2])
        send_on(order[1])
        pass_on(order[3])
        send_on(order[2])

        def finish(half, ref):
            slot = z * 2 + half
            total = gather(z, half)

            @pl.when(z == 0)
            def _():
                sink(z, half).wait_recv()
                ref[...] = (total + f32(from_above.at[slot])).astype(jnp.bfloat16)

            @pl.when(z == Z - 1)
            def _():
                rise(z, half).wait_recv()
                ref[...] = (total + f32(from_below.at[slot])).astype(jnp.bfloat16)

            @pl.when((z > 0) & (z < Z - 1))
            def _():
                sink(z, half).wait_recv()
                rise(z, half).wait_recv()
                ref[...] = (total + f32(from_above.at[slot]) + f32(from_below.at[slot])).astype(jnp.bfloat16)

        finish(1 - core, final)
        hand_over().start()
        finish(core, out)
        for level in order:
            for half in (0, 1):
                home_cross(level, half).wait_send()
                pl.when(level < z)(lambda: sink(level, half).wait_send())
                pl.when(level > z)(lambda: rise(level, half).wait_send())
        hand_over().wait_send()


def reduce_rows(term, block, tokens):
    dma = pltpu.SemaphoreType.DMA

    def pieces(count):
        return pltpu.VMEM((count, block, tokens), jnp.bfloat16)

    one = pltpu.VMEM((block, tokens), jnp.bfloat16)
    return pl.pallas_call(
        functools.partial(reduce_kernel, block),
        out_shape=jax.ShapeDtypeStruct((block, tokens), jnp.bfloat16),
        in_specs=[VMEM],
        out_specs=VMEM,
        scratch_shapes=[
            pieces(12), pieces(8), pieces(8), pieces(8), pieces(4), pieces(8), one, one,
            dma((12,)), dma((8,)), dma((8,)), dma((8,)), dma,
            dma((4,)), dma((4,)), dma((12,)), dma((8,)), dma,
        ],
        compiler_params=pltpu.CompilerParams(
            collective_id=1, has_side_effects=True, vmem_limit_bytes=VMEM_BYTES
        ),
    )(term)


def per_device_chips(n, hidden, head_weight, labels, loss_weight):
    tokens, block = hidden.shape
    features, logit_grad, token_loss = forward(
        hidden.T, head_weight, labels.reshape(1, tokens), loss_weight.reshape(1, tokens), n
    )
    term = lax.dot_general(
        head_weight, logit_grad, (((0,), (0,)), ((), ())), preferred_element_type=jnp.float32
    ).astype(jnp.bfloat16)
    hidden_grad = reduce_rows(term, block, tokens).T
    head_grad = lax.dot_general(
        logit_grad, features, (((1,), (1,)), ((), ())), preferred_element_type=jnp.float32
    ).astype(jnp.bfloat16)
    return hidden_grad, head_grad, token_loss.reshape(tokens)


def per_device(hidden, head_weight, labels, loss_weight):
    tokens = hidden.shape[0]
    rows = head_weight.shape[0]
    features = lax.all_gather(hidden, GROUP, axis=1, tiled=True)
    features = lax.all_to_all(features, "dp", split_axis=1, concat_axis=0, tiled=True)
    partial = lax.dot_general(
        head_weight, features, (((1,), (1,)), ((), ())), preferred_element_type=jnp.float32
    )
    logits = lax.psum_scatter(partial, "dp", scatter_dimension=1, tiled=True)
    entries = lax.axis_index(GROUP) * rows + jnp.arange(rows, dtype=jnp.int32)
    mask = (entries[:, None] == labels[None, :]).astype(jnp.float32)
    row_peak = lax.pmax(jnp.max(logits, axis=0), GROUP)
    shifted_exp = jnp.exp(logits - row_peak[None, :])
    row_total, picked = lax.psum((jnp.sum(shifted_exp, axis=0), jnp.sum(mask * logits, axis=0)), GROUP)
    token_loss = row_peak + jnp.log(row_total) - picked
    grad = (loss_weight[None, :] * (shifted_exp / row_total[None, :] - mask)).astype(jnp.bfloat16)
    grad = lax.all_gather(grad, "dp", axis=1, tiled=True)
    head_grad = jnp.dot(grad, features, preferred_element_type=jnp.float32).astype(jnp.bfloat16)
    term = lax.dot_general(grad, head_weight, (((0,), (0,)), ((), ())), preferred_element_type=jnp.float32)
    term = lax.all_to_all(term, "dp", split_axis=0, concat_axis=1, tiled=True)
    hidden_grad = lax.psum_scatter(term, GROUP, scatter_dimension=1, tiled=True).astype(jnp.bfloat16)
    return hidden_grad, head_grad, token_loss


def solution(mesh):
    sizes = dict(mesh.shape)
    if (sizes["pipe"], sizes["tensor"], sizes["dp"]) == (4, Z, 2):
        body = functools.partial(per_device_chips, 4 * Z)
    else:
        body = per_device
    return jax.shard_map(
        body,
        mesh=mesh,
        in_specs=(P("dp", GROUP), P(GROUP, "dp"), P("dp"), P("dp")),
        out_specs=(P("dp", GROUP), P(GROUP, "dp"), P("dp")),
        check_vma=False,
    )
```

```python
import functools

import jax
import jax.numpy as jnp
from jax import lax
from jax.experimental import pallas as pl
from jax.experimental.pallas import tpu as pltpu
from jax.sharding import PartitionSpec as P

GROUP = ("pipe", "tensor")
MESH = pl.DeviceIdType.MESH
VMEM = pl.BlockSpec(memory_space=pltpu.VMEM)
ANY = pl.BlockSpec(memory_space=pl.ANY)
HBM = pl.BlockSpec(memory_space=pltpu.HBM)
VMEM_BYTES = 48 * 1024 * 1024
Z = 4


def spans(rows, size):
    return [(start, min(size, rows - start)) for start in range(0, rows, size)]


class Place:
    def __init__(self):
        pipe = lax.axis_index("pipe")
        self.pipe = pipe
        self.x, self.y = pipe % 2, pipe // 2
        self.z = lax.axis_index("tensor")
        self.core = lax.axis_index("dp")
        self.home = self.y == self.core
        self.away = self.y == 1 - self.core
        self.x_peer = {"pipe": self.y * 2 + 1 - self.x}
        self.y_peer = {"pipe": (1 - self.y) * 2 + self.x}
        self.up = {"tensor": self.z + 1}
        self.down = {"tensor": self.z - 1}
        self.mate = {"dp": 1 - self.core}


def remote(src, dst, send_sem, recv_sem, device):
    return pltpu.make_async_remote_copy(
        src_ref=src, dst_ref=dst, send_sem=send_sem, recv_sem=recv_sem, device_id=device, device_id_type=MESH
    )


def greet_group(me, n):
    barrier = pltpu.get_barrier_semaphore()
    index = me.pipe * Z + me.z

    def greet(step, carry):
        other = (index + step) % n
        pl.semaphore_signal(
            barrier, inc=1, device_id={"pipe": other // Z, "tensor": other % Z}, device_id_type=MESH
        )
        return carry

    lax.fori_loop(1, n, greet, 0)
    pl.semaphore_signal(barrier, inc=1, device_id=me.mate, device_id_type=MESH)
    pl.semaphore_wait(barrier, n)


def head_kernel(
    n, block, piece, weight, labels_in, loss_weight_in,
    features_out, grad_out, loss_out, hidden_out,
    features, weight_here, partial, partial_in, grads, term, stats, labels, loss_weight,
    recv, recv_low, send_up, send_down, low_up, low_down, send_x, send_y, send_y2, own_sem, weight_sem,
    mate_sems, stat_send, stat_recv, out_sems, token_sems, *reduce_scratch
):
    me = Place()
    tokens = piece.shape[1]
    rows = weight.shape[0]
    x, z, core = me.x, me.z, me.core
    load_weight = pltpu.make_async_copy(weight, weight_here, weight_sem)
    load_weight.start()
    load_tokens = [
        pltpu.make_async_copy(labels_in, labels, token_sems.at[0]),
        pltpu.make_async_copy(loss_weight_in, loss_weight, token_sems.at[1]),
    ]
    for load in load_tokens:
        load.start()
    greet_group(me, n)
    low = block // 80 * 16
    whole, upper, lower = (0, block), (low, block - low), (0, low)

    def at(column, level, half, part):
        start = pl.multiple_of((column * Z + level) * block + part[0], 16)
        return features.at[pl.ds(start, part[1]), pl.ds(pl.multiple_of(half * tokens, tokens), tokens)]

    def copy(column, level, half, send_sem, device, part):
        here = at(column, level, half, part)
        sems = recv_low if part is lower else recv
        return remote(here, here, send_sem, sems.at[(column * Z + level) * 2 + half], device)

    def arrived(column, level, half, part):
        copy(column, level, half, send_y.at[0], me.mate, part).wait_recv()

    def run(transfer):
        if waiting:
            transfer.wait_send()
        else:
            transfer.start()

    def need(column, level, half, part):
        if not waiting:
            arrived(column, level, half, part)

    def line_sends(level, half, sign, part):
        slot = level * 2 + half
        if sign <= 0:
            pl.when(z < Z - 1)(lambda: run(copy(x, level, half, send_up.at[slot], me.up, upper)))
        if sign >= 0:
            pl.when(z > 0)(lambda: run(copy(x, level, half, send_down.at[slot], me.down, upper)))
        run(copy(x, level, half, send_x.at[slot], me.x_peer, part))
        run(copy(x, level, half, send_y.at[slot], me.y_peer, part))

    def line_step(distance, sign):
        level = z + sign * distance

        def home():
            for half in (core, 1 - core):
                need(x, level, half, upper)
                line_sends(level, half, sign, upper)

        def away():
            need(x, level, 0, upper)
            run(copy(x, level, 0, send_x.at[level * 2], me.x_peer, upper))
            need(x, level, 1, upper)

        valid = (level >= 0) & (level < Z)
        pl.when(valid & me.home)(home)
        pl.when(valid & me.away)(away)

    def first_step():
        @pl.when(me.home)
        def _():
            line_sends(z, core, 0, whole)
            need(x, z, 1 - core, whole)
            line_sends(z, 1 - core, 0, whole)

        @pl.when(me.away)
        def _():
            need(x, z, 0, whole)
            run(copy(x, z, 0, send_x.at[z * 2], me.x_peer, whole))
            need(x, z, 1, whole)

    def peer_step(distance, sign):
        level = z + sign * distance
        part = upper if distance else whole
        valid = (level >= 0) & (level < Z)
        if not waiting:
            @pl.when(valid)
            def _():
                arrived(1 - x, level, 0, part)
                arrived(1 - x, level, 1, part)

        pl.when(valid & me.home)(
            lambda: run(copy(1 - x, level, 1, send_y2.at[level], me.y_peer, part))
        )

    def low_step(distance, sign):
        level = z + sign * distance

        def each(which, carry):
            column, half = which // 2, which % 2
            slot = (column * Z + level) * 2 + half
            if distance:
                need(column, level, half, lower)
            if sign <= 0:
                pl.when(z < Z - 1)(lambda: run(copy(column, level, half, low_up.at[slot], me.up, lower)))
            if sign >= 0:
                pl.when(z > 0)(lambda: run(copy(column, level, half, low_down.at[slot], me.down, lower)))
            return carry

        @pl.when((level >= 0) & (level < Z))
        def _():
            lax.fori_loop(0, 4, each, 0)

    def multiply(pair, half, first):
        width = 2 * block
        depth = pl.ds(pl.multiple_of(pair * width, width), width)
        right = features[depth, pl.ds(pl.multiple_of(half * tokens, tokens), tokens)]
        for start, size in spans(rows, 592):
            part = jnp.dot(weight_here[pl.ds(start, size), depth], right, preferred_element_type=jnp.float32)
            where = (half, pl.ds(start, size))
            partial[where] = part if first else partial[where] + part

    def multiply_both(pair, first=False):
        def step(half, carry):
            multiply(pair, half, first)
            return carry

        lax.fori_loop(0, 2, step, 0)

    waiting = False
    mine = at(x, z, core, whole)
    own_copy = pltpu.make_async_copy(piece, mine, own_sem)
    own_send = remote(piece, mine, own_sem, recv.at[(x * Z + z) * 2 + core], me.mate)
    pl.when(me.home)(own_copy.start)
    pl.when(me.away)(own_send.start)
    pl.when(me.home)(own_copy.wait)
    first_step()
    for sign in (-1, 1):
        line_step(1, sign)
    peer_step(0, 1)
    low_step(0, 0)
    for sign in (-1, 1):
        line_step(2, sign)
    for sign in (-1, 1):
        peer_step(1, sign)
    for sign in (-1, 1):
        low_step(1, sign)
    load_weight.wait()
    multiply_both(x * 2 + z // 2, True)
    for sign in (-1, 1):
        line_step(3, sign)
    for sign in (-1, 1):
        peer_step(2, sign)
    for sign in (-1, 1):
        low_step(2, sign)
    multiply_both((1 - x) * 2 + z // 2)
    for sign in (-1, 1):
        peer_step(3, sign)
    for sign in (-1, 1):
        low_step(3, sign)
    store_features = pltpu.make_async_copy(features, features_out, out_sems.at[0])
    store_features.start()
    near, far = x * 2 + 1 - z // 2, (1 - x) * 2 + 1 - z // 2
    multiply(near, 1 - core, False)
    multiply(far, 1 - core, False)
    swap = remote(partial.at[1 - core], partial_in, mate_sems.at[0], mate_sems.at[1], me.mate)
    swap.start()
    multiply(near, core, False)
    multiply(far, core, False)

    waiting = True
    pl.when(me.away)(own_send.wait_send)
    first_step()
    peer_step(0, 1)
    low_step(0, 0)
    for distance in (1, 2, 3):
        for sign in (-1, 1):
            line_step(distance, sign)
            peer_step(distance, sign)
            low_step(distance, sign)
    for load in load_tokens:
        load.wait()
    swap.wait()

    index = me.pipe * Z + z
    target = labels[...] - index * rows
    peak = jnp.full((1, tokens), -jnp.inf, jnp.float32)
    picked = jnp.zeros((1, tokens), jnp.float32)
    parts = spans(rows, 128)

    def is_target(start, size):
        return lax.broadcasted_iota(jnp.int32, (size, tokens), 0) + start == target

    for start, size in parts:
        where = pl.ds(start, size)
        logits = partial[core, where] + partial_in[where]
        partial_in[where] = logits
        peak = jnp.maximum(peak, jnp.max(logits, axis=0, keepdims=True))
        picked += jnp.sum(jnp.where(is_target(start, size), logits, 0.0), axis=0, keepdims=True)
    total = jnp.zeros((1, tokens), jnp.float32)
    for start, size in parts:
        total += jnp.sum(jnp.exp(partial_in[pl.ds(start, size)] - peak), axis=0, keepdims=True)
    stats[index] = jnp.concatenate([peak, total, picked, jnp.zeros((5, tokens), jnp.float32)], axis=0)

    def stat_copy(step):
        other = (index + step) % n
        device = {"pipe": other // Z, "tensor": other % Z}
        return remote(stats.at[index], stats.at[index], stat_send.at[step], stat_recv.at[index], device)

    def send_stat(step, carry):
        stat_copy(step).start()
        return carry

    def wait_stat(step, carry):
        other = (index + step) % n
        remote(
            stats.at[other], stats.at[other], stat_send.at[step], stat_recv.at[other], me.mate
        ).wait_recv()
        return carry

    def wait_stat_send(step, carry):
        stat_copy(step).wait_send()
        return carry

    lax.fori_loop(1, n, send_stat, 0)
    lax.fori_loop(1, n, wait_stat, 0)
    every = stats[...]
    peaks, totals, picks = every[:, 0], every[:, 1], every[:, 2]
    row_peak = jnp.max(peaks, axis=0, keepdims=True)
    row_total = jnp.sum(totals * jnp.exp(peaks - row_peak), axis=0, keepdims=True)
    loss_out[...] = row_peak + jnp.log(row_total) - jnp.sum(picks, axis=0, keepdims=True)
    scale = loss_weight[...]
    inverse = 1.0 / row_total
    for start, size in parts:
        where = pl.ds(start, size)
        share = jnp.exp(partial_in[where] - row_peak) * inverse
        hit = jnp.where(is_target(start, size), 1.0, 0.0)
        grads[core, where] = (scale * (share - hit)).astype(jnp.bfloat16)
    share_grad = remote(grads.at[core], grads.at[core], mate_sems.at[2], mate_sems.at[3], me.mate)
    share_grad.start()

    def keep(half, sem):
        there = grad_out.at[:, pl.ds(pl.multiple_of(half * tokens, tokens), tokens)]
        return pltpu.make_async_copy(grads.at[half], there, sem)

    keep(core, out_sems.at[1]).start()

    def multiply_back(pair, half):
        width = 2 * block
        depth = pl.ds(pl.multiple_of(pair * width, width), width)
        term[depth, pl.ds(pl.multiple_of(half * tokens, tokens), tokens)] = lax.dot_general(
            weight_here[:, depth], grads[half], (((0,), (0,)), ((), ())), preferred_element_type=jnp.float32
        ).astype(jnp.bfloat16)

    def back(step, carry):
        multiply_back(jnp.where(step % 2 == 0, far, near), jnp.where(step < 2, core, 1 - core))
        return carry

    def back_rest(step, carry):
        column = jnp.where(step % 2 == 0, 1 - x, x)
        multiply_back(column * 2 + z // 2, step // 2)
        return carry

    lax.fori_loop(0, 2, back, 0)
    share_grad.wait_recv()
    keep(1 - core, out_sems.at[2]).start()
    lax.fori_loop(2, 4, back, 0)
    reduce_rows(me, block, term, hidden_out, lambda: lax.fori_loop(0, 4, back_rest, 0), *reduce_scratch)

    lax.fori_loop(1, n, wait_stat_send, 0)
    share_grad.wait_send()
    keep(core, out_sems.at[1]).wait()
    keep(1 - core, out_sems.at[2]).wait()
    store_features.wait()


def head(hidden_t, head_weight, labels, loss_weight, n):
    block, tokens = hidden_t.shape
    rows, width = head_weight.shape
    dma = pltpu.SemaphoreType.DMA

    def pieces(count):
        return pltpu.VMEM((count, block, tokens), jnp.bfloat16)

    one = pltpu.VMEM((block, tokens), jnp.bfloat16)
    return pl.pallas_call(
        functools.partial(head_kernel, n, block),
        out_shape=(
            jax.ShapeDtypeStruct((width, 2 * tokens), jnp.bfloat16),
            jax.ShapeDtypeStruct((rows, 2 * tokens), jnp.bfloat16),
            jax.ShapeDtypeStruct((1, tokens), jnp.float32),
            jax.ShapeDtypeStruct((block, tokens), jnp.bfloat16),
        ),
        in_specs=[HBM, ANY, HBM, HBM],
        out_specs=(ANY, ANY, VMEM, VMEM),
        scratch_shapes=[
            pltpu.VMEM((width, 2 * tokens), jnp.bfloat16),
            pltpu.VMEM((rows, width), jnp.bfloat16),
            pltpu.VMEM((2, rows, tokens), jnp.float32),
            pltpu.VMEM((rows, tokens), jnp.float32),
            pltpu.VMEM((2, rows, tokens), jnp.bfloat16),
            pltpu.VMEM((width, 2 * tokens), jnp.bfloat16),
            pltpu.VMEM((n, 8, tokens), jnp.float32),
            pltpu.VMEM((1, tokens), jnp.int32),
            pltpu.VMEM((1, tokens), jnp.float32),
            dma((16,)), dma((16,)), dma((8,)), dma((8,)), dma((16,)), dma((16,)), dma((8,)), dma((8,)), dma((4,)),
            dma, dma, dma((4,)), dma((n,)), dma((n,)), dma((3,)), dma((2,)),
            pieces(12), pieces(8), pieces(8), pieces(8), pieces(4), pieces(8), one, one,
            dma((12,)), dma((8,)), dma((8,)), dma((8,)), dma,
            dma((4,)), dma((4,)), dma((12,)), dma((8,)), dma,
        ],
        compiler_params=pltpu.CompilerParams(
            collective_id=0, has_side_effects=True, vmem_limit_bytes=VMEM_BYTES
        ),
    )(hidden_t, head_weight, labels, loss_weight)


def reduce_rows(
    me, block, term, out, finish_term,
    from_y, from_x, from_below, from_above, passed, summed, final, landed,
    recv_y, recv_x, recv_below, recv_above, recv_final,
    send_x, send_pass, send_y, send_z, send_final,
):
    tokens = out.shape[1]
    x, z, core = me.x, me.z, me.core

    def own(column, level, half):
        start = pl.multiple_of((column * Z + level) * block, block)
        return term.at[pl.ds(start, block), pl.ds(pl.multiple_of(half * tokens, tokens), tokens)]

    upper = z // 2
    order = (3 * (1 - upper), 2 - upper, 1 - z + 4 * upper, z)

    def away_cross(level):
        return remote(own(1 - x, level, 0), from_x.at[level * 2], send_x.at[level], recv_x.at[level * 2], me.x_peer)

    def away_diagonal(level):
        return remote(own(1 - x, level, 1), from_y.at[8 + level], send_y.at[8 + level], recv_y.at[8 + level], me.y_peer)

    def away_line(level, half):
        slot = level * 2 + half
        source = own(x, level, 1) if half else passed.at[level]
        return remote(source, from_y.at[slot], send_y.at[slot], recv_y.at[slot], me.y_peer)

    def home_cross(level, half):
        slot = level * 2 + half
        source = passed.at[level] if half else own(1 - x, level, 0)
        sem = send_pass.at[level] if half else send_x.at[level]
        return remote(source, from_x.at[slot], sem, recv_x.at[slot], me.x_peer)

    def rise(level, half):
        slot = level * 2 + half
        return remote(summed.at[slot], from_below.at[slot], send_z.at[slot], recv_below.at[slot], me.up)

    def sink(level, half):
        slot = level * 2 + half
        return remote(summed.at[slot], from_above.at[slot], send_z.at[slot], recv_above.at[slot], me.down)

    def hand_over():
        return remote(final, landed, send_final, recv_final, me.mate)

    def f32(ref):
        return ref[...].astype(jnp.float32)

    @pl.when(me.away)
    def _():
        for level in order[:2]:
            away_cross(level).start()
            away_diagonal(level).start()
            away_line(level, 1).start()

    @pl.when(me.home)
    def _():
        for level in order[:2]:
            home_cross(level, 0).start()

    finish_term()

    @pl.when(me.away)
    def _():
        for at, level in enumerate(order):
            away_cross(level).wait_recv()
            passed[level] = (f32(own(x, level, 0)) + f32(from_x.at[level * 2])).astype(jnp.bfloat16)
            away_line(level, 0).start()
            if at + 2 < Z:
                away_cross(order[at + 2]).start()
                away_diagonal(order[at + 2]).start()
                away_line(order[at + 2], 1).start()
        for level in order:
            away_cross(level).wait_send()
            away_diagonal(level).wait_send()
            away_line(level, 1).wait_send()
            away_line(level, 0).wait_send()
        hand_over().wait_recv()
        out[...] = landed[...]

    @pl.when(me.home)
    def _():
        def pass_on(level):
            away_diagonal(level).wait_recv()
            passed[level] = (f32(own(1 - x, level, 1)) + f32(from_y.at[8 + level])).astype(jnp.bfloat16)
            home_cross(level, 1).start()

        def gather(level, half):
            slot = level * 2 + half
            for inbox, sems in ((from_y, recv_y), (from_x, recv_x)):
                remote(final, inbox.at[slot], send_final, sems.at[slot], me.mate).wait_recv()
            return f32(own(x, level, half)) + f32(from_y.at[slot]) + f32(from_x.at[slot])

        def send_on(level):
            for half in (1, 0):
                slot = level * 2 + half
                total = gather(level, half)
                summed[slot] = total.astype(jnp.bfloat16)

                @pl.when((level < z) & (z < Z - 1))
                def _():
                    sink(level, half).wait_recv()
                    summed[slot] = (total + f32(from_above.at[slot])).astype(jnp.bfloat16)

                @pl.when((level > z) & (z > 0))
                def _():
                    rise(level, half).wait_recv()
                    summed[slot] = (total + f32(from_below.at[slot])).astype(jnp.bfloat16)

                pl.when(level < z)(lambda: sink(level, half).start())
                pl.when(level > z)(lambda: rise(level, half).start())

        pass_on(order[0])
        home_cross(order[2], 0).start()
        pass_on(order[1])
        send_on(order[0])
        home_cross(order[3], 0).start()
        pass_on(order[2])
        send_on(order[1])
        pass_on(order[3])
        send_on(order[2])

        def finish(half, ref):
            slot = z * 2 + half
            total = gather(z, half)

            @pl.when(z == 0)
            def _():
                sink(z, half).wait_recv()
                ref[...] = (total + f32(from_above.at[slot])).astype(jnp.bfloat16)

            @pl.when(z == Z - 1)
            def _():
                rise(z, half).wait_recv()
                ref[...] = (total + f32(from_below.at[slot])).astype(jnp.bfloat16)

            @pl.when((z > 0) & (z < Z - 1))
            def _():
                sink(z, half).wait_recv()
                rise(z, half).wait_recv()
                ref[...] = (total + f32(from_above.at[slot]) + f32(from_below.at[slot])).astype(jnp.bfloat16)

        finish(1 - core, final)
        hand_over().start()
        finish(core, out)
        for level in order:
            for half in (0, 1):
                home_cross(level, half).wait_send()
                pl.when(level < z)(lambda: sink(level, half).wait_send())
                pl.when(level > z)(lambda: rise(level, half).wait_send())
        hand_over().wait_send()


def per_device_chips(n, hidden, head_weight, labels, loss_weight):
    tokens, block = hidden.shape
    features, logit_grad, token_loss, hidden_grad = head(
        hidden.T, head_weight, labels.reshape(1, tokens), loss_weight.reshape(1, tokens), n
    )
    head_grad = lax.dot_general(
        logit_grad, features, (((1,), (1,)), ((), ())), preferred_element_type=jnp.float32
    ).astype(jnp.bfloat16)
    return hidden_grad.T, head_grad, token_loss.reshape(tokens)


def per_device(hidden, head_weight, labels, loss_weight):
    tokens = hidden.shape[0]
    rows = head_weight.shape[0]
    features = lax.all_gather(hidden, GROUP, axis=1, tiled=True)
    features = lax.all_to_all(features, "dp", split_axis=1, concat_axis=0, tiled=True)
    partial = lax.dot_general(
        head_weight, features, (((1,), (1,)), ((), ())), preferred_element_type=jnp.float32
    )
    logits = lax.psum_scatter(partial, "dp", scatter_dimension=1, tiled=True)
    entries = lax.axis_index(GROUP) * rows + jnp.arange(rows, dtype=jnp.int32)
    mask = (entries[:, None] == labels[None, :]).astype(jnp.float32)
    row_peak = lax.pmax(jnp.max(logits, axis=0), GROUP)
    shifted_exp = jnp.exp(logits - row_peak[None, :])
    row_total, picked = lax.psum((jnp.sum(shifted_exp, axis=0), jnp.sum(mask * logits, axis=0)), GROUP)
    token_loss = row_peak + jnp.log(row_total) - picked
    grad = (loss_weight[None, :] * (shifted_exp / row_total[None, :] - mask)).astype(jnp.bfloat16)
    grad = lax.all_gather(grad, "dp", axis=1, tiled=True)
    head_grad = jnp.dot(grad, features, preferred_element_type=jnp.float32).astype(jnp.bfloat16)
    term = lax.dot_general(grad, head_weight, (((0,), (0,)), ((), ())), preferred_element_type=jnp.float32)
    term = lax.all_to_all(term, "dp", split_axis=0, concat_axis=1, tiled=True)
    hidden_grad = lax.psum_scatter(term, GROUP, scatter_dimension=1, tiled=True).astype(jnp.bfloat16)
    return hidden_grad, head_grad, token_loss


def solution(mesh):
    sizes = dict(mesh.shape)
    if (sizes["pipe"], sizes["tensor"], sizes["dp"]) == (4, Z, 2):
        body = functools.partial(per_device_chips, 4 * Z)
    else:
        body = per_device
    return jax.shard_map(
        body,
        mesh=mesh,
        in_specs=(P("dp", GROUP), P(GROUP, "dp"), P("dp"), P("dp")),
        out_specs=(P("dp", GROUP), P(GROUP, "dp"), P("dp")),
        check_vma=False,
    )
```

```python
import functools

import jax
import jax.numpy as jnp
from jax import lax
from jax.experimental import pallas as pl
from jax.experimental.pallas import tpu as pltpu
from jax.sharding import PartitionSpec as P

GROUP = ("pipe", "tensor")
MESH = pl.DeviceIdType.MESH
VMEM = pl.BlockSpec(memory_space=pltpu.VMEM)
ANY = pl.BlockSpec(memory_space=pl.ANY)
HBM = pl.BlockSpec(memory_space=pltpu.HBM)
VMEM_BYTES = 48 * 1024 * 1024
Z = 4


def spans(rows, size):
    return [(start, min(size, rows - start)) for start in range(0, rows, size)]


class Place:
    def __init__(self):
        pipe = lax.axis_index("pipe")
        self.pipe = pipe
        self.x, self.y = pipe % 2, pipe // 2
        self.z = lax.axis_index("tensor")
        self.core = lax.axis_index("dp")
        self.home = self.y == self.core
        self.away = self.y == 1 - self.core
        self.x_peer = {"pipe": self.y * 2 + 1 - self.x}
        self.y_peer = {"pipe": (1 - self.y) * 2 + self.x}
        self.mate = {"dp": 1 - self.core}


def remote(src, dst, send_sem, recv_sem, device):
    return pltpu.make_async_remote_copy(
        src_ref=src, dst_ref=dst, send_sem=send_sem, recv_sem=recv_sem, device_id=device, device_id_type=MESH
    )


def greet_group(me, n):
    barrier = pltpu.get_barrier_semaphore()
    index = me.pipe * Z + me.z

    def greet(step, carry):
        other = (index + step) % n
        pl.semaphore_signal(
            barrier, inc=1, device_id={"pipe": other // Z, "tensor": other % Z}, device_id_type=MESH
        )
        return carry

    lax.fori_loop(1, n, greet, 0)
    pl.semaphore_signal(barrier, inc=1, device_id=me.mate, device_id_type=MESH)
    pl.semaphore_wait(barrier, n)


def head_kernel(
    n, block, piece, weight, labels_in, loss_weight_in,
    features_out, grad_out, loss_out, hidden_out,
    features, weight_here, partial, partial_in, grads, term, stats, labels, loss_weight,
    recv, send_z, send_x, send_y, send_y2, own_sem, weight_sem,
    swap_send, swap_recv, mate_sems, stat_send, stat_recv, out_sems, token_sems, *reduce_scratch
):
    me = Place()
    tokens = piece.shape[1]
    rows = weight.shape[0]
    x, z, core = me.x, me.z, me.core
    load_weight = pltpu.make_async_copy(weight, weight_here, weight_sem)
    load_weight.start()
    load_tokens = [
        pltpu.make_async_copy(labels_in, labels, token_sems.at[0]),
        pltpu.make_async_copy(loss_weight_in, loss_weight, token_sems.at[1]),
    ]
    for load in load_tokens:
        load.start()
    greet_group(me, n)

    def at(column, level, half):
        start = pl.multiple_of((column * Z + level) * block, block)
        return features.at[pl.ds(start, block), pl.ds(pl.multiple_of(half * tokens, tokens), tokens)]

    def copy(column, level, half, send_sem, device):
        here = at(column, level, half)
        return remote(here, here, send_sem, recv.at[(column * Z + level) * 2 + half], device)

    def run(transfer):
        if waiting:
            transfer.wait_send()
        else:
            transfer.start()

    def need(column, level, half):
        if not waiting:
            copy(column, level, half, send_y.at[0], me.mate).wait_recv()

    def line_sends(level, half):
        slot = level * 2 + half
        run(copy(x, level, half, send_x.at[slot], me.x_peer))
        run(copy(x, level, half, send_y.at[slot], me.y_peer))

    def own_sends(half):
        for step in range(1, Z):
            other = (z + step) % Z
            run(copy(x, z, half, send_z.at[other * 2 + half], {"tensor": other}))
        line_sends(z, half)

    def line_step(distance, sign):
        level = z + sign * distance

        def home():
            for half in (core, 1 - core):
                need(x, level, half)
                line_sends(level, half)

        def away():
            need(x, level, 0)
            run(copy(x, level, 0, send_x.at[level * 2], me.x_peer))
            need(x, level, 1)

        valid = (level >= 0) & (level < Z)
        pl.when(valid & me.home)(home)
        pl.when(valid & me.away)(away)

    def first_step():
        @pl.when(me.home)
        def _():
            own_sends(core)
            need(x, z, 1 - core)
            own_sends(1 - core)

        @pl.when(me.away)
        def _():
            need(x, z, 0)
            run(copy(x, z, 0, send_x.at[z * 2], me.x_peer))
            need(x, z, 1)

    def peer_step(distance, sign):
        level = z + sign * distance

        @pl.when((level >= 0) & (level < Z))
        def _():
            need(1 - x, level, 1)
            pl.when(me.home)(lambda: run(copy(1 - x, level, 1, send_y2.at[level], me.y_peer)))
            need(1 - x, level, 0)

    cuts = spans(rows, 608)

    def multiply(pair, half, first, cut):
        width = 2 * block
        depth = pl.ds(pl.multiple_of(pair * width, width), width)
        right = features[depth, pl.ds(pl.multiple_of(half * tokens, tokens), tokens)]
        part = jnp.dot(weight_here[pl.ds(*cut), depth], right, preferred_element_type=jnp.float32)
        where = (half, pl.ds(*cut))
        partial[where] = part if first else partial[where] + part

    def multiply_both(pair, first=False):
        def step(half, carry):
            for cut in cuts:
                multiply(pair, half, first, cut)
            return carry

        lax.fori_loop(0, 2, step, 0)

    waiting = False
    mine = at(x, z, core)
    own_copy = pltpu.make_async_copy(piece, mine, own_sem)
    own_send = remote(piece, mine, own_sem, recv.at[(x * Z + z) * 2 + core], me.mate)
    pl.when(me.home)(own_copy.start)
    pl.when(me.away)(own_send.start)
    pl.when(me.home)(own_copy.wait)
    near, far = x * 2 + 1 - z // 2, (1 - x) * 2 + 1 - z // 2

    def both(step, distance):
        for sign in (-1, 1):
            step(distance, sign)

    first_step()
    both(line_step, 1)
    peer_step(0, 1)
    both(line_step, 2)
    both(line_step, 3)
    load_weight.wait()
    multiply_both(x * 2 + z // 2, True)
    both(peer_step, 1)
    multiply_both(near)
    both(peer_step, 2)
    multiply_both((1 - x) * 2 + z // 2)
    both(peer_step, 3)
    store_features = pltpu.make_async_copy(features, features_out, out_sems.at[0])
    store_features.start()
    swaps = []
    for at_cut, (start, size) in enumerate(cuts):
        multiply(far, 1 - core, False, (start, size))
        sent = pl.ds(start, -(-size // 8) * 8)
        swaps.append(remote(
            partial.at[1 - core, sent], partial_in.at[sent],
            swap_send.at[at_cut], swap_recv.at[at_cut], me.mate,
        ))
        swaps[-1].start()
    for cut in cuts:
        multiply(far, core, False, cut)

    waiting = True
    pl.when(me.away)(own_send.wait_send)
    first_step()
    peer_step(0, 1)
    for distance in (1, 2, 3):
        both(line_step, distance)
        both(peer_step, distance)
    for load in load_tokens:
        load.wait()

    index = me.pipe * Z + z
    target = labels[...] - index * rows
    peak = jnp.full((1, tokens), -jnp.inf, jnp.float32)
    picked = jnp.zeros((1, tokens), jnp.float32)
    parts = [
        (cut + start, size) for cut, length in cuts for start, size in spans(length, 128)
    ]

    def is_target(start, size):
        return lax.broadcasted_iota(jnp.int32, (size, tokens), 0) + start == target

    for start, size in parts:
        for swap, cut in zip(swaps, cuts):
            if start == cut[0]:
                swap.wait_recv()
        where = pl.ds(start, size)
        logits = partial[core, where] + partial_in[where]
        partial_in[where] = logits
        peak = jnp.maximum(peak, jnp.max(logits, axis=0, keepdims=True))
        picked += jnp.sum(jnp.where(is_target(start, size), logits, 0.0), axis=0, keepdims=True)
    total = jnp.zeros((1, tokens), jnp.float32)
    for start, size in parts:
        total += jnp.sum(jnp.exp(partial_in[pl.ds(start, size)] - peak), axis=0, keepdims=True)
    stats[index] = jnp.concatenate([peak, total, picked, jnp.zeros((5, tokens), jnp.float32)], axis=0)

    def stat_copy(step):
        other = (index + step) % n
        device = {"pipe": other // Z, "tensor": other % Z}
        return remote(stats.at[index], stats.at[index], stat_send.at[step], stat_recv.at[index], device)

    def send_stat(step, carry):
        stat_copy(step).start()
        return carry

    def wait_stat(step, carry):
        other = (index + step) % n
        remote(
            stats.at[other], stats.at[other], stat_send.at[step], stat_recv.at[other], me.mate
        ).wait_recv()
        return carry

    def wait_stat_send(step, carry):
        stat_copy(step).wait_send()
        return carry

    lax.fori_loop(1, n, send_stat, 0)
    lax.fori_loop(1, n, wait_stat, 0)
    every = stats[...]
    peaks, totals, picks = every[:, 0], every[:, 1], every[:, 2]
    row_peak = jnp.max(peaks, axis=0, keepdims=True)
    row_total = jnp.sum(totals * jnp.exp(peaks - row_peak), axis=0, keepdims=True)
    loss_out[...] = row_peak + jnp.log(row_total) - jnp.sum(picks, axis=0, keepdims=True)
    scale = loss_weight[...]
    inverse = 1.0 / row_total
    for start, size in parts:
        where = pl.ds(start, size)
        share = jnp.exp(partial_in[where] - row_peak) * inverse
        hit = jnp.where(is_target(start, size), 1.0, 0.0)
        grads[core, where] = (scale * (share - hit)).astype(jnp.bfloat16)
    share_grad = remote(grads.at[core], grads.at[core], mate_sems.at[0], mate_sems.at[1], me.mate)
    share_grad.start()

    def keep(half, sem):
        there = grad_out.at[:, pl.ds(pl.multiple_of(half * tokens, tokens), tokens)]
        return pltpu.make_async_copy(grads.at[half], there, sem)

    keep(core, out_sems.at[1]).start()

    def multiply_back(pair, half):
        width = 2 * block
        depth = pl.ds(pl.multiple_of(pair * width, width), width)
        term[depth, pl.ds(pl.multiple_of(half * tokens, tokens), tokens)] = lax.dot_general(
            weight_here[:, depth], grads[half], (((0,), (0,)), ((), ())), preferred_element_type=jnp.float32
        ).astype(jnp.bfloat16)

    def back(step, carry):
        multiply_back(jnp.where(step % 2 == 0, far, near), jnp.where(step < 2, core, 1 - core))
        return carry

    def back_rest(step, carry):
        column = jnp.where(step % 2 == 0, 1 - x, x)
        multiply_back(column * 2 + z // 2, step // 2)
        return carry

    lax.fori_loop(0, 2, back, 0)
    share_grad.wait_recv()
    keep(1 - core, out_sems.at[2]).start()
    lax.fori_loop(2, 4, back, 0)
    reduce_rows(me, block, term, hidden_out, lambda: lax.fori_loop(0, 4, back_rest, 0), *reduce_scratch)

    lax.fori_loop(1, n, wait_stat_send, 0)
    for swap in swaps:
        swap.wait_send()
    share_grad.wait_send()
    keep(core, out_sems.at[1]).wait()
    keep(1 - core, out_sems.at[2]).wait()
    store_features.wait()


def head(hidden_t, head_weight, labels, loss_weight, n):
    block, tokens = hidden_t.shape
    rows, width = head_weight.shape
    padded = -(-rows // 8) * 8
    dma = pltpu.SemaphoreType.DMA

    def pieces(count):
        return pltpu.VMEM((count, block, tokens), jnp.bfloat16)

    one = pltpu.VMEM((block, tokens), jnp.bfloat16)
    return pl.pallas_call(
        functools.partial(head_kernel, n, block),
        out_shape=(
            jax.ShapeDtypeStruct((width, 2 * tokens), jnp.bfloat16),
            jax.ShapeDtypeStruct((rows, 2 * tokens), jnp.bfloat16),
            jax.ShapeDtypeStruct((1, tokens), jnp.float32),
            jax.ShapeDtypeStruct((block, tokens), jnp.bfloat16),
        ),
        in_specs=[HBM, ANY, HBM, HBM],
        out_specs=(ANY, ANY, VMEM, VMEM),
        scratch_shapes=[
            pltpu.VMEM((width, 2 * tokens), jnp.bfloat16),
            pltpu.VMEM((rows, width), jnp.bfloat16),
            pltpu.VMEM((2, padded, tokens), jnp.float32),
            pltpu.VMEM((padded, tokens), jnp.float32),
            pltpu.VMEM((2, rows, tokens), jnp.bfloat16),
            pltpu.VMEM((width, 2 * tokens), jnp.bfloat16),
            pltpu.VMEM((n, 8, tokens), jnp.float32),
            pltpu.VMEM((1, tokens), jnp.int32),
            pltpu.VMEM((1, tokens), jnp.float32),
            dma((16,)), dma((8,)), dma((8,)), dma((8,)), dma((4,)), dma, dma,
            dma((2,)), dma((2,)), dma((2,)), dma((n,)), dma((n,)), dma((3,)), dma((2,)),
            pieces(12), pieces(8), pieces(8), pieces(4), pieces(8), one, one,
            dma((12,)), dma((8,)), dma((8,)), dma,
            dma((4,)), dma((4,)), dma((12,)), dma((8,)), dma,
        ],
        compiler_params=pltpu.CompilerParams(
            collective_id=0, has_side_effects=True, vmem_limit_bytes=VMEM_BYTES
        ),
    )(hidden_t, head_weight, labels, loss_weight)


def reduce_rows(
    me, block, term, out, finish_term,
    from_y, from_x, from_z, passed, summed, final, landed,
    recv_y, recv_x, recv_z, recv_final,
    send_x, send_pass, send_y, send_z, send_final,
):
    tokens = out.shape[1]
    x, z, core = me.x, me.z, me.core

    def own(column, level, half):
        start = pl.multiple_of((column * Z + level) * block, block)
        return term.at[pl.ds(start, block), pl.ds(pl.multiple_of(half * tokens, tokens), tokens)]

    upper = z // 2
    order = (3 * (1 - upper), 2 - upper, 1 - z + 4 * upper, z)

    def away_cross(level):
        return remote(own(1 - x, level, 0), from_x.at[level * 2], send_x.at[level], recv_x.at[level * 2], me.x_peer)

    def away_diagonal(level):
        return remote(own(1 - x, level, 1), from_y.at[8 + level], send_y.at[8 + level], recv_y.at[8 + level], me.y_peer)

    def away_line(level, half):
        slot = level * 2 + half
        source = own(x, level, 1) if half else passed.at[level]
        return remote(source, from_y.at[slot], send_y.at[slot], recv_y.at[slot], me.y_peer)

    def home_cross(level, half):
        slot = level * 2 + half
        source = passed.at[level] if half else own(1 - x, level, 0)
        sem = send_pass.at[level] if half else send_x.at[level]
        return remote(source, from_x.at[slot], sem, recv_x.at[slot], me.x_peer)

    def along(level, half):
        slot, source = level * 2 + half, z * 2 + half
        return remote(
            summed.at[slot], from_z.at[source], send_z.at[slot], recv_z.at[source], {"tensor": level}
        )

    def hand_over():
        return remote(final, landed, send_final, recv_final, me.mate)

    def f32(ref):
        return ref[...].astype(jnp.float32)

    @pl.when(me.away)
    def _():
        for level in order[:2]:
            away_cross(level).start()
            away_diagonal(level).start()
            away_line(level, 1).start()

    @pl.when(me.home)
    def _():
        for level in order[:2]:
            home_cross(level, 0).start()

    finish_term()

    @pl.when(me.away)
    def _():
        for at, level in enumerate(order):
            away_cross(level).wait_recv()
            passed[level] = (f32(own(x, level, 0)) + f32(from_x.at[level * 2])).astype(jnp.bfloat16)
            away_line(level, 0).start()
            if at + 2 < Z:
                away_cross(order[at + 2]).start()
                away_diagonal(order[at + 2]).start()
                away_line(order[at + 2], 1).start()
        for level in order:
            away_cross(level).wait_send()
            away_diagonal(level).wait_send()
            away_line(level, 1).wait_send()
            away_line(level, 0).wait_send()
        hand_over().wait_recv()
        out[...] = landed[...]

    @pl.when(me.home)
    def _():
        def pass_on(level):
            away_diagonal(level).wait_recv()
            passed[level] = (f32(own(1 - x, level, 1)) + f32(from_y.at[8 + level])).astype(jnp.bfloat16)
            home_cross(level, 1).start()

        def gather(level, half):
            slot = level * 2 + half
            for inbox, sems in ((from_y, recv_y), (from_x, recv_x)):
                remote(final, inbox.at[slot], send_final, sems.at[slot], me.mate).wait_recv()
            return f32(own(x, level, half)) + f32(from_y.at[slot]) + f32(from_x.at[slot])

        def send_on(level):
            for half in (1, 0):
                summed[level * 2 + half] = gather(level, half).astype(jnp.bfloat16)
                along(level, half).start()

        pass_on(order[0])
        home_cross(order[2], 0).start()
        pass_on(order[1])
        send_on(order[0])
        home_cross(order[3], 0).start()
        pass_on(order[2])
        send_on(order[1])
        pass_on(order[3])
        send_on(order[2])

        def finish(half, ref):
            total = gather(z, half)
            for step in range(1, Z):
                slot = (z + step) % Z * 2 + half
                remote(final, from_z.at[slot], send_final, recv_z.at[slot], me.mate).wait_recv()
                total += f32(from_z.at[slot])
            ref[...] = total.astype(jnp.bfloat16)

        finish(1 - core, final)
        hand_over().start()
        finish(core, out)
        for level in order:
            for half in (0, 1):
                home_cross(level, half).wait_send()
        for level in order[:3]:
            for half in (0, 1):
                along(level, half).wait_send()
        hand_over().wait_send()


def per_device_chips(n, hidden, head_weight, labels, loss_weight):
    tokens, block = hidden.shape
    features, logit_grad, token_loss, hidden_grad = head(
        hidden.T, head_weight, labels.reshape(1, tokens), loss_weight.reshape(1, tokens), n
    )
    head_grad = lax.dot_general(
        logit_grad, features, (((1,), (1,)), ((), ())), preferred_element_type=jnp.float32
    ).astype(jnp.bfloat16)
    return hidden_grad.T, head_grad, token_loss.reshape(tokens)


def per_device(hidden, head_weight, labels, loss_weight):
    tokens = hidden.shape[0]
    rows = head_weight.shape[0]
    features = lax.all_gather(hidden, GROUP, axis=1, tiled=True)
    features = lax.all_to_all(features, "dp", split_axis=1, concat_axis=0, tiled=True)
    partial = lax.dot_general(
        head_weight, features, (((1,), (1,)), ((), ())), preferred_element_type=jnp.float32
    )
    logits = lax.psum_scatter(partial, "dp", scatter_dimension=1, tiled=True)
    entries = lax.axis_index(GROUP) * rows + jnp.arange(rows, dtype=jnp.int32)
    mask = (entries[:, None] == labels[None, :]).astype(jnp.float32)
    row_peak = lax.pmax(jnp.max(logits, axis=0), GROUP)
    shifted_exp = jnp.exp(logits - row_peak[None, :])
    row_total, picked = lax.psum((jnp.sum(shifted_exp, axis=0), jnp.sum(mask * logits, axis=0)), GROUP)
    token_loss = row_peak + jnp.log(row_total) - picked
    grad = (loss_weight[None, :] * (shifted_exp / row_total[None, :] - mask)).astype(jnp.bfloat16)
    grad = lax.all_gather(grad, "dp", axis=1, tiled=True)
    head_grad = jnp.dot(grad, features, preferred_element_type=jnp.float32).astype(jnp.bfloat16)
    term = lax.dot_general(grad, head_weight, (((0,), (0,)), ((), ())), preferred_element_type=jnp.float32)
    term = lax.all_to_all(term, "dp", split_axis=0, concat_axis=1, tiled=True)
    hidden_grad = lax.psum_scatter(term, GROUP, scatter_dimension=1, tiled=True).astype(jnp.bfloat16)
    return hidden_grad, head_grad, token_loss


def solution(mesh):
    sizes = dict(mesh.shape)
    if (sizes["pipe"], sizes["tensor"], sizes["dp"]) == (4, Z, 2):
        body = functools.partial(per_device_chips, 4 * Z)
    else:
        body = per_device
    return jax.shard_map(
        body,
        mesh=mesh,
        in_specs=(P("dp", GROUP), P(GROUP, "dp"), P("dp"), P("dp")),
        out_specs=(P("dp", GROUP), P(GROUP, "dp"), P("dp")),
        check_vma=False,
    )
```

```python
import functools

import jax
import jax.numpy as jnp
from jax import lax
from jax.experimental import pallas as pl
from jax.experimental.pallas import tpu as pltpu
from jax.sharding import PartitionSpec as P

GROUP = ("pipe", "tensor")
MESH = pl.DeviceIdType.MESH
VMEM = pl.BlockSpec(memory_space=pltpu.VMEM)
ANY = pl.BlockSpec(memory_space=pl.ANY)
HBM = pl.BlockSpec(memory_space=pltpu.HBM)
VMEM_BYTES = 48 * 1024 * 1024
Z = 4


def spans(rows, size):
    return [(start, min(size, rows - start)) for start in range(0, rows, size)]


class Place:
    def __init__(self):
        pipe = lax.axis_index("pipe")
        self.pipe = pipe
        self.x, self.y = pipe % 2, pipe // 2
        self.z = lax.axis_index("tensor")
        self.core = lax.axis_index("dp")
        self.home = self.y == self.core
        self.away = self.y == 1 - self.core
        self.x_peer = {"pipe": self.y * 2 + 1 - self.x}
        self.y_peer = {"pipe": (1 - self.y) * 2 + self.x}
        self.up = {"tensor": self.z + 1}
        self.down = {"tensor": self.z - 1}
        self.mate = {"dp": 1 - self.core}


def remote(src, dst, send_sem, recv_sem, device):
    return pltpu.make_async_remote_copy(
        src_ref=src, dst_ref=dst, send_sem=send_sem, recv_sem=recv_sem, device_id=device, device_id_type=MESH
    )


def greet_group(me, n):
    barrier = pltpu.get_barrier_semaphore()
    index = me.pipe * Z + me.z

    def greet(step, carry):
        other = (index + step) % n
        pl.semaphore_signal(
            barrier, inc=1, device_id={"pipe": other // Z, "tensor": other % Z}, device_id_type=MESH
        )
        return carry

    lax.fori_loop(1, n, greet, 0)
    pl.semaphore_signal(barrier, inc=1, device_id=me.mate, device_id_type=MESH)
    pl.semaphore_wait(barrier, n)


def head_kernel(
    n, block, piece, weight, labels_in, loss_weight_in,
    features_out, grad_out, loss_out, hidden_out,
    features, weight_here, partial, partial_in, grads, term, stats, labels, loss_weight,
    recv, recv_low, send_up, send_down, low_up, low_down, send_x, send_y, send_y2, own_sem, weight_sem,
    swap_send, swap_recv, mate_sems, stat_send, stat_recv, out_sems, token_sems, *reduce_scratch
):
    me = Place()
    tokens = piece.shape[1]
    rows = weight.shape[0]
    x, z, core = me.x, me.z, me.core
    load_weight = pltpu.make_async_copy(weight, weight_here, weight_sem)
    load_weight.start()
    load_tokens = [
        pltpu.make_async_copy(labels_in, labels, token_sems.at[0]),
        pltpu.make_async_copy(loss_weight_in, loss_weight, token_sems.at[1]),
    ]
    for load in load_tokens:
        load.start()
    greet_group(me, n)
    low = block // 80 * 16
    whole, upper, lower = (0, block), (low, block - low), (0, low)

    def at(column, level, half, part):
        start = pl.multiple_of((column * Z + level) * block + part[0], 16)
        return features.at[pl.ds(start, part[1]), pl.ds(pl.multiple_of(half * tokens, tokens), tokens)]

    def copy(column, level, half, send_sem, device, part):
        here = at(column, level, half, part)
        sems = recv_low if part is lower else recv
        return remote(here, here, send_sem, sems.at[(column * Z + level) * 2 + half], device)

    def arrived(column, level, half, part):
        copy(column, level, half, send_y.at[0], me.mate, part).wait_recv()

    def run(transfer):
        if waiting:
            transfer.wait_send()
        else:
            transfer.start()

    def need(column, level, half, part):
        if not waiting:
            arrived(column, level, half, part)

    def line_sends(level, half, sign, part):
        slot = level * 2 + half
        if sign <= 0:
            pl.when(z < Z - 1)(lambda: run(copy(x, level, half, send_up.at[slot], me.up, upper)))
        if sign >= 0:
            pl.when(z > 0)(lambda: run(copy(x, level, half, send_down.at[slot], me.down, upper)))
        run(copy(x, level, half, send_x.at[slot], me.x_peer, part))
        run(copy(x, level, half, send_y.at[slot], me.y_peer, part))

    def line_step(distance, sign):
        level = z + sign * distance

        def home():
            for half in (core, 1 - core):
                need(x, level, half, upper)
                line_sends(level, half, sign, upper)

        def away():
            need(x, level, 0, upper)
            run(copy(x, level, 0, send_x.at[level * 2], me.x_peer, upper))
            need(x, level, 1, upper)

        valid = (level >= 0) & (level < Z)
        pl.when(valid & me.home)(home)
        pl.when(valid & me.away)(away)

    def first_step():
        @pl.when(me.home)
        def _():
            line_sends(z, core, 0, whole)
            need(x, z, 1 - core, whole)
            line_sends(z, 1 - core, 0, whole)

        @pl.when(me.away)
        def _():
            need(x, z, 0, whole)
            run(copy(x, z, 0, send_x.at[z * 2], me.x_peer, whole))
            need(x, z, 1, whole)

    def peer_step(distance, sign):
        level = z + sign * distance
        part = upper if distance else whole
        valid = (level >= 0) & (level < Z)
        if not waiting:
            @pl.when(valid)
            def _():
                arrived(1 - x, level, 0, part)
                arrived(1 - x, level, 1, part)

        pl.when(valid & me.home)(
            lambda: run(copy(1 - x, level, 1, send_y2.at[level], me.y_peer, part))
        )

    def low_step(distance, sign):
        level = z + sign * distance

        def each(which, carry):
            column, half = which // 2, which % 2
            slot = (column * Z + level) * 2 + half
            if distance:
                need(column, level, half, lower)
            if sign <= 0:
                pl.when(z < Z - 1)(lambda: run(copy(column, level, half, low_up.at[slot], me.up, lower)))
            if sign >= 0:
                pl.when(z > 0)(lambda: run(copy(column, level, half, low_down.at[slot], me.down, lower)))
            return carry

        @pl.when((level >= 0) & (level < Z))
        def _():
            lax.fori_loop(0, 4, each, 0)

    cuts = spans(rows, 608)

    def multiply(pair, half, first, cut):
        width = 2 * block
        depth = pl.ds(pl.multiple_of(pair * width, width), width)
        right = features[depth, pl.ds(pl.multiple_of(half * tokens, tokens), tokens)]
        part = jnp.dot(weight_here[pl.ds(*cut), depth], right, preferred_element_type=jnp.float32)
        where = (half, pl.ds(*cut))
        partial[where] = part if first else partial[where] + part

    def multiply_both(pair, first=False):
        def step(half, carry):
            for cut in cuts:
                multiply(pair, half, first, cut)
            return carry

        lax.fori_loop(0, 2, step, 0)

    waiting = False
    mine = at(x, z, core, whole)
    own_copy = pltpu.make_async_copy(piece, mine, own_sem)
    own_send = remote(piece, mine, own_sem, recv.at[(x * Z + z) * 2 + core], me.mate)
    pl.when(me.home)(own_copy.start)
    pl.when(me.away)(own_send.start)
    pl.when(me.home)(own_copy.wait)
    first_step()
    for sign in (-1, 1):
        line_step(1, sign)
    peer_step(0, 1)
    low_step(0, 0)
    for sign in (-1, 1):
        line_step(2, sign)
    for sign in (-1, 1):
        peer_step(1, sign)
    for sign in (-1, 1):
        low_step(1, sign)
    load_weight.wait()
    multiply_both(x * 2 + z // 2, True)
    for sign in (-1, 1):
        line_step(3, sign)
    for sign in (-1, 1):
        peer_step(2, sign)
    for sign in (-1, 1):
        low_step(2, sign)
    multiply_both((1 - x) * 2 + z // 2)
    for sign in (-1, 1):
        peer_step(3, sign)
    for sign in (-1, 1):
        low_step(3, sign)
    store_features = pltpu.make_async_copy(features, features_out, out_sems.at[0])
    store_features.start()
    near, far = x * 2 + 1 - z // 2, (1 - x) * 2 + 1 - z // 2
    swaps = []
    for at_cut, (start, size) in enumerate(cuts):
        multiply(near, 1 - core, False, (start, size))
        multiply(far, 1 - core, False, (start, size))
        sent = pl.ds(start, -(-size // 8) * 8)
        swaps.append(remote(
            partial.at[1 - core, sent], partial_in.at[sent],
            swap_send.at[at_cut], swap_recv.at[at_cut], me.mate,
        ))
        swaps[-1].start()
    for cut in cuts:
        multiply(near, core, False, cut)
        multiply(far, core, False, cut)

    waiting = True
    pl.when(me.away)(own_send.wait_send)
    first_step()
    peer_step(0, 1)
    low_step(0, 0)
    for distance in (1, 2, 3):
        for sign in (-1, 1):
            line_step(distance, sign)
            peer_step(distance, sign)
            low_step(distance, sign)
    for load in load_tokens:
        load.wait()

    index = me.pipe * Z + z
    target = labels[...] - index * rows
    peak = jnp.full((1, tokens), -jnp.inf, jnp.float32)
    picked = jnp.zeros((1, tokens), jnp.float32)
    parts = [
        (cut + start, size) for cut, length in cuts for start, size in spans(length, 128)
    ]

    def is_target(start, size):
        return lax.broadcasted_iota(jnp.int32, (size, tokens), 0) + start == target

    for start, size in parts:
        for swap, cut in zip(swaps, cuts):
            if start == cut[0]:
                swap.wait_recv()
        where = pl.ds(start, size)
        logits = partial[core, where] + partial_in[where]
        partial_in[where] = logits
        peak = jnp.maximum(peak, jnp.max(logits, axis=0, keepdims=True))
        picked += jnp.sum(jnp.where(is_target(start, size), logits, 0.0), axis=0, keepdims=True)
    total = jnp.zeros((1, tokens), jnp.float32)
    for start, size in parts:
        total += jnp.sum(jnp.exp(partial_in[pl.ds(start, size)] - peak), axis=0, keepdims=True)
    stats[index] = jnp.concatenate([peak, total, picked, jnp.zeros((5, tokens), jnp.float32)], axis=0)

    def stat_copy(step):
        other = (index + step) % n
        device = {"pipe": other // Z, "tensor": other % Z}
        return remote(stats.at[index], stats.at[index], stat_send.at[step], stat_recv.at[index], device)

    def send_stat(step, carry):
        stat_copy(step).start()
        return carry

    def wait_stat(step, carry):
        other = (index + step) % n
        remote(
            stats.at[other], stats.at[other], stat_send.at[step], stat_recv.at[other], me.mate
        ).wait_recv()
        return carry

    def wait_stat_send(step, carry):
        stat_copy(step).wait_send()
        return carry

    lax.fori_loop(1, n, send_stat, 0)
    lax.fori_loop(1, n, wait_stat, 0)
    every = stats[...]
    peaks, totals, picks = every[:, 0], every[:, 1], every[:, 2]
    row_peak = jnp.max(peaks, axis=0, keepdims=True)
    row_total = jnp.sum(totals * jnp.exp(peaks - row_peak), axis=0, keepdims=True)
    loss_out[...] = row_peak + jnp.log(row_total) - jnp.sum(picks, axis=0, keepdims=True)
    scale = loss_weight[...]
    inverse = 1.0 / row_total
    for start, size in parts:
        where = pl.ds(start, size)
        share = jnp.exp(partial_in[where] - row_peak) * inverse
        hit = jnp.where(is_target(start, size), 1.0, 0.0)
        grads[core, where] = (scale * (share - hit)).astype(jnp.bfloat16)
    share_grad = remote(grads.at[core], grads.at[core], mate_sems.at[0], mate_sems.at[1], me.mate)
    share_grad.start()

    def keep(half, sem):
        there = grad_out.at[:, pl.ds(pl.multiple_of(half * tokens, tokens), tokens)]
        return pltpu.make_async_copy(grads.at[half], there, sem)

    keep(core, out_sems.at[1]).start()

    def multiply_back(pair, half):
        width = 2 * block
        depth = pl.ds(pl.multiple_of(pair * width, width), width)
        term[depth, pl.ds(pl.multiple_of(half * tokens, tokens), tokens)] = lax.dot_general(
            weight_here[:, depth], grads[half], (((0,), (0,)), ((), ())), preferred_element_type=jnp.float32
        ).astype(jnp.bfloat16)

    def back(step, carry):
        multiply_back(jnp.where(step % 2 == 0, far, near), jnp.where(step < 2, core, 1 - core))
        return carry

    def back_rest(step, carry):
        column = jnp.where(step % 2 == 0, 1 - x, x)
        multiply_back(column * 2 + z // 2, step // 2)
        return carry

    lax.fori_loop(0, 2, back, 0)
    share_grad.wait_recv()
    keep(1 - core, out_sems.at[2]).start()
    lax.fori_loop(2, 4, back, 0)
    reduce_rows(me, block, term, hidden_out, lambda: lax.fori_loop(0, 4, back_rest, 0), *reduce_scratch)

    lax.fori_loop(1, n, wait_stat_send, 0)
    for swap in swaps:
        swap.wait_send()
    share_grad.wait_send()
    keep(core, out_sems.at[1]).wait()
    keep(1 - core, out_sems.at[2]).wait()
    store_features.wait()


def head(hidden_t, head_weight, labels, loss_weight, n):
    block, tokens = hidden_t.shape
    rows, width = head_weight.shape
    padded = -(-rows // 8) * 8
    low = block // 100 * 16
    dma = pltpu.SemaphoreType.DMA

    def pieces(count):
        return pltpu.VMEM((count, block, tokens), jnp.bfloat16)

    one = pltpu.VMEM((block, tokens), jnp.bfloat16)
    return pl.pallas_call(
        functools.partial(head_kernel, n, block),
        out_shape=(
            jax.ShapeDtypeStruct((width, 2 * tokens), jnp.bfloat16),
            jax.ShapeDtypeStruct((rows, 2 * tokens), jnp.bfloat16),
            jax.ShapeDtypeStruct((1, tokens), jnp.float32),
            jax.ShapeDtypeStruct((block, tokens), jnp.bfloat16),
        ),
        in_specs=[HBM, ANY, HBM, HBM],
        out_specs=(ANY, ANY, VMEM, VMEM),
        scratch_shapes=[
            pltpu.VMEM((width, 2 * tokens), jnp.bfloat16),
            pltpu.VMEM((rows, width), jnp.bfloat16),
            pltpu.VMEM((2, padded, tokens), jnp.float32),
            pltpu.VMEM((padded, tokens), jnp.float32),
            pltpu.VMEM((2, rows, tokens), jnp.bfloat16),
            pltpu.VMEM((width, 2 * tokens), jnp.bfloat16),
            pltpu.VMEM((n, 8, tokens), jnp.float32),
            pltpu.VMEM((1, tokens), jnp.int32),
            pltpu.VMEM((1, tokens), jnp.float32),
            dma((16,)), dma((16,)), dma((8,)), dma((8,)), dma((16,)), dma((16,)), dma((8,)), dma((8,)), dma((4,)),
            dma, dma, dma((2,)), dma((2,)), dma((2,)), dma((n,)), dma((n,)), dma((3,)), dma((2,)),
            pieces(12), pieces(8), pieces(8), pieces(8), pieces(4), pieces(8), one, one,
            pltpu.VMEM((16, low, tokens), jnp.bfloat16), pieces(4),
            dma((12,)), dma((8,)), dma((8,)), dma((8,)), dma, dma((16,)), dma((16,)),
            dma((4,)), dma((4,)), dma((12,)), dma((8,)), dma,
        ],
        compiler_params=pltpu.CompilerParams(
            collective_id=0, has_side_effects=True, vmem_limit_bytes=VMEM_BYTES
        ),
    )(hidden_t, head_weight, labels, loss_weight)


def reduce_rows(
    me, block, term, out, finish_term,
    from_y, from_x, from_below, from_above, passed, summed, final, landed, from_low, at_home,
    recv_y, recv_x, recv_below, recv_above, recv_final, recv_low, send_low,
    send_x, send_pass, send_y, send_z, send_final,
):
    tokens = out.shape[1]
    x, z, core = me.x, me.z, me.core

    low = from_low.shape[1]
    whole, upper, lower = (0, block), (low, block - low), (0, low)

    top = z // 2
    order = (3 * (1 - top), 2 - top, 1 - z + 4 * top, z)
    last = Z - 1

    def own(column, level, half, part):
        start = pl.multiple_of((column * Z + level) * block + part[0], 16)
        return term.at[pl.ds(start, part[1]), pl.ds(pl.multiple_of(half * tokens, tokens), tokens)]

    def cut(ref, turn, slot):
        start, size = whole if turn == last else upper
        return ref.at[slot, pl.ds(start, size)]

    def mine(peer, turn, half):
        if turn == last:
            return at_home.at[peer * 2 + half]
        return own(1 - x if peer else x, order[turn], half, upper)

    def away_cross(turn):
        level = order[turn]
        slot = level * 2
        return remote(mine(1, turn, 0), cut(from_x, turn, slot), send_x.at[level], recv_x.at[slot], me.x_peer)

    def away_diagonal(turn):
        slot = 8 + order[turn]
        return remote(mine(1, turn, 1), cut(from_y, turn, slot), send_y.at[slot], recv_y.at[slot], me.y_peer)

    def away_line(turn, half):
        slot = order[turn] * 2 + half
        source = mine(0, turn, 1) if half else cut(passed, turn, order[turn])
        return remote(source, cut(from_y, turn, slot), send_y.at[slot], recv_y.at[slot], me.y_peer)

    def home_cross(turn, half):
        level = order[turn]
        slot = level * 2 + half
        source = cut(passed, turn, level) if half else mine(1, turn, 0)
        sem = send_pass.at[level] if half else send_x.at[level]
        return remote(source, cut(from_x, turn, slot), sem, recv_x.at[slot], me.x_peer)

    def rise(level, half):
        slot = level * 2 + half
        return remote(cut(summed, 0, slot), cut(from_below, 0, slot), send_z.at[slot], recv_below.at[slot], me.up)

    def sink(level, half):
        slot = level * 2 + half
        return remote(cut(summed, 0, slot), cut(from_above, 0, slot), send_z.at[slot], recv_above.at[slot], me.down)

    def low_copy(turn, which):
        level = order[turn]
        source = own(x + which // 2 * (1 - 2 * x), level, which % 2, lower)
        slot, there = z * 4 + which, level * 4 + which
        return remote(source, from_low.at[slot], send_low.at[there], recv_low.at[slot], {"tensor": level})

    def each_low(act):
        def step(which, carry):
            act(which)
            return carry

        lax.fori_loop(0, 4, step, 0)

    def settle(which):
        column, half = x + which // 2 * (1 - 2 * x), which % 2
        total = f32(own(column, z, half, lower))
        for step in range(1, Z):
            slot = (z + step) % Z * 4 + which
            here = from_low.at[slot]
            remote(here, here, send_final, recv_low.at[slot], me.mate).wait_recv()
            total += f32(here)
        at_home[which, pl.ds(0, low)] = total.astype(jnp.bfloat16)
        at_home[which, pl.ds(low, block - low)] = own(column, z, half, upper)[...]

    def hand_over():
        return remote(final, landed, send_final, recv_final, me.mate)

    def f32(ref):
        return ref[...].astype(jnp.float32)

    for turn in (0, 1):
        each_low(lambda which: low_copy(turn, which).start())

    @pl.when(me.away)
    def _():
        for turn in (0, 1):
            away_cross(turn).start()
            away_diagonal(turn).start()
            away_line(turn, 1).start()

    @pl.when(me.home)
    def _():
        for turn in (0, 1):
            home_cross(turn, 0).start()

    finish_term()
    each_low(lambda which: low_copy(2, which).start())

    def away_turn(turn):
        level = order[turn]
        away_cross(turn).wait_recv()
        cut(passed, turn, level)[...] = (
            f32(mine(0, turn, 0)) + f32(cut(from_x, turn, level * 2))
        ).astype(jnp.bfloat16)
        away_line(turn, 0).start()
        if turn + 2 < Z:
            away_cross(turn + 2).start()
            away_diagonal(turn + 2).start()
            away_line(turn + 2, 1).start()

    def pass_on(turn):
        level = order[turn]
        away_diagonal(turn).wait_recv()
        cut(passed, turn, level)[...] = (
            f32(mine(1, turn, 1)) + f32(cut(from_y, turn, 8 + level))
        ).astype(jnp.bfloat16)
        home_cross(turn, 1).start()

    def gather(turn, half):
        slot = order[turn] * 2 + half
        total = f32(mine(0, turn, half))
        for inbox, sems in ((from_y, recv_y), (from_x, recv_x)):
            here = cut(inbox, turn, slot)
            remote(here, here, send_final, sems.at[slot], me.mate).wait_recv()
            total += f32(here)
        return total

    def send_on(turn):
        level = order[turn]
        for half in (1, 0):
            slot = level * 2 + half
            total = gather(turn, half)
            kept = cut(summed, turn, slot)
            kept[...] = total.astype(jnp.bfloat16)

            @pl.when((level < z) & (z < Z - 1))
            def _():
                sink(level, half).wait_recv()
                kept[...] = (total + f32(cut(from_above, turn, slot))).astype(jnp.bfloat16)

            @pl.when((level > z) & (z > 0))
            def _():
                rise(level, half).wait_recv()
                kept[...] = (total + f32(cut(from_below, turn, slot))).astype(jnp.bfloat16)

            pl.when(level < z)(lambda: sink(level, half).start())
            pl.when(level > z)(lambda: rise(level, half).start())

    def finish(half, ref):
        slot = z * 2 + half
        total = gather(last, half)
        ref[pl.ds(0, low)] = total[:low].astype(jnp.bfloat16)
        rest, there = total[low:], pl.ds(low, block - low)
        above, below = cut(from_above, 0, slot), cut(from_below, 0, slot)

        @pl.when(z == 0)
        def _():
            sink(z, half).wait_recv()
            ref[there] = (rest + f32(above)).astype(jnp.bfloat16)

        @pl.when(z == Z - 1)
        def _():
            rise(z, half).wait_recv()
            ref[there] = (rest + f32(below)).astype(jnp.bfloat16)

        @pl.when((z > 0) & (z < Z - 1))
        def _():
            sink(z, half).wait_recv()
            rise(z, half).wait_recv()
            ref[there] = (rest + f32(above) + f32(below)).astype(jnp.bfloat16)

    pl.when(me.away)(lambda: away_turn(0))

    @pl.when(me.home)
    def _():
        pass_on(0)
        home_cross(2, 0).start()
        pass_on(1)

    each_low(settle)

    @pl.when(me.away)
    def _():
        for turn in (1, 2, 3):
            away_turn(turn)
        for turn in range(Z):
            away_cross(turn).wait_send()
            away_diagonal(turn).wait_send()
            away_line(turn, 1).wait_send()
            away_line(turn, 0).wait_send()
        hand_over().wait_recv()
        out[...] = landed[...]

    @pl.when(me.home)
    def _():
        send_on(0)
        home_cross(3, 0).start()
        pass_on(2)
        send_on(1)
        pass_on(3)
        send_on(2)
        finish(1 - core, final)
        hand_over().start()
        finish(core, out)
        for turn in range(Z):
            level = order[turn]
            for half in (0, 1):
                home_cross(turn, half).wait_send()
                if turn < last:
                    pl.when(level < z)(lambda: sink(level, half).wait_send())
                    pl.when(level > z)(lambda: rise(level, half).wait_send())
        hand_over().wait_send()

    for turn in range(last):
        each_low(lambda which: low_copy(turn, which).wait_send())


def per_device_chips(n, hidden, head_weight, labels, loss_weight):
    tokens, block = hidden.shape
    features, logit_grad, token_loss, hidden_grad = head(
        hidden.T, head_weight, labels.reshape(1, tokens), loss_weight.reshape(1, tokens), n
    )
    head_grad = lax.dot_general(
        logit_grad, features, (((1,), (1,)), ((), ())), preferred_element_type=jnp.float32
    ).astype(jnp.bfloat16)
    return hidden_grad.T, head_grad, token_loss.reshape(tokens)


def per_device(hidden, head_weight, labels, loss_weight):
    tokens = hidden.shape[0]
    rows = head_weight.shape[0]
    features = lax.all_gather(hidden, GROUP, axis=1, tiled=True)
    features = lax.all_to_all(features, "dp", split_axis=1, concat_axis=0, tiled=True)
    partial = lax.dot_general(
        head_weight, features, (((1,), (1,)), ((), ())), preferred_element_type=jnp.float32
    )
    logits = lax.psum_scatter(partial, "dp", scatter_dimension=1, tiled=True)
    entries = lax.axis_index(GROUP) * rows + jnp.arange(rows, dtype=jnp.int32)
    mask = (entries[:, None] == labels[None, :]).astype(jnp.float32)
    row_peak = lax.pmax(jnp.max(logits, axis=0), GROUP)
    shifted_exp = jnp.exp(logits - row_peak[None, :])
    row_total, picked = lax.psum((jnp.sum(shifted_exp, axis=0), jnp.sum(mask * logits, axis=0)), GROUP)
    token_loss = row_peak + jnp.log(row_total) - picked
    grad = (loss_weight[None, :] * (shifted_exp / row_total[None, :] - mask)).astype(jnp.bfloat16)
    grad = lax.all_gather(grad, "dp", axis=1, tiled=True)
    head_grad = jnp.dot(grad, features, preferred_element_type=jnp.float32).astype(jnp.bfloat16)
    term = lax.dot_general(grad, head_weight, (((0,), (0,)), ((), ())), preferred_element_type=jnp.float32)
    term = lax.all_to_all(term, "dp", split_axis=0, concat_axis=1, tiled=True)
    hidden_grad = lax.psum_scatter(term, GROUP, scatter_dimension=1, tiled=True).astype(jnp.bfloat16)
    return hidden_grad, head_grad, token_loss


def solution(mesh):
    sizes = dict(mesh.shape)
    if (sizes["pipe"], sizes["tensor"], sizes["dp"]) == (4, Z, 2):
        body = functools.partial(per_device_chips, 4 * Z)
    else:
        body = per_device
    return jax.shard_map(
        body,
        mesh=mesh,
        in_specs=(P("dp", GROUP), P(GROUP, "dp"), P("dp"), P("dp")),
        out_specs=(P("dp", GROUP), P(GROUP, "dp"), P("dp")),
        check_vma=False,
    )
```

```python
import functools

import jax
import jax.numpy as jnp
from jax import lax
from jax.experimental import pallas as pl
from jax.experimental.pallas import tpu as pltpu
from jax.sharding import PartitionSpec as P

GROUP = ("pipe", "tensor")
MESH = pl.DeviceIdType.MESH
VMEM = pl.BlockSpec(memory_space=pltpu.VMEM)
ANY = pl.BlockSpec(memory_space=pl.ANY)
HBM = pl.BlockSpec(memory_space=pltpu.HBM)
VMEM_BYTES = 48 * 1024 * 1024
Z = 4


def spans(rows, size):
    return [(start, min(size, rows - start)) for start in range(0, rows, size)]


class Place:
    def __init__(self):
        pipe = lax.axis_index("pipe")
        self.pipe = pipe
        self.x, self.y = pipe % 2, pipe // 2
        self.z = lax.axis_index("tensor")
        self.core = lax.axis_index("dp")
        self.home = self.y == self.core
        self.away = self.y == 1 - self.core
        self.x_peer = {"pipe": self.y * 2 + 1 - self.x}
        self.y_peer = {"pipe": (1 - self.y) * 2 + self.x}
        self.up = {"tensor": self.z + 1}
        self.down = {"tensor": self.z - 1}
        self.mate = {"dp": 1 - self.core}


def remote(src, dst, send_sem, recv_sem, device):
    return pltpu.make_async_remote_copy(
        src_ref=src, dst_ref=dst, send_sem=send_sem, recv_sem=recv_sem, device_id=device, device_id_type=MESH
    )


def greet_group(me, n):
    barrier = pltpu.get_barrier_semaphore()
    index = me.pipe * Z + me.z

    def greet(step, carry):
        other = (index + step) % n
        pl.semaphore_signal(
            barrier, inc=1, device_id={"pipe": other // Z, "tensor": other % Z}, device_id_type=MESH
        )
        return carry

    lax.fori_loop(1, n, greet, 0)
    pl.semaphore_signal(barrier, inc=1, device_id=me.mate, device_id_type=MESH)
    pl.semaphore_wait(barrier, n)


def head_kernel(
    n, block, piece, weight, labels_in, loss_weight_in,
    features_out, grad_out, loss_out, hidden_out,
    features, weight_here, partial, partial_in, grads, term, stats, labels, loss_weight,
    recv, recv_low, send_up, send_down, low_up, low_down, send_x, send_y, send_y2, own_sem, weight_sem,
    swap_send, swap_recv, mate_sems, stat_send, stat_recv, out_sems, token_sems, *reduce_scratch
):
    me = Place()
    tokens = piece.shape[1]
    rows = weight.shape[0]
    x, z, core = me.x, me.z, me.core
    load_weight = pltpu.make_async_copy(weight, weight_here, weight_sem)
    load_weight.start()
    load_tokens = [
        pltpu.make_async_copy(labels_in, labels, token_sems.at[0]),
        pltpu.make_async_copy(loss_weight_in, loss_weight, token_sems.at[1]),
    ]
    for load in load_tokens:
        load.start()
    greet_group(me, n)
    low = block // 80 * 16
    whole, upper, lower = (0, block), (low, block - low), (0, low)

    def at(column, level, half, part):
        start = pl.multiple_of((column * Z + level) * block + part[0], 16)
        return features.at[pl.ds(start, part[1]), pl.ds(pl.multiple_of(half * tokens, tokens), tokens)]

    def copy(column, level, half, send_sem, device, part):
        here = at(column, level, half, part)
        sems = recv_low if part is lower else recv
        return remote(here, here, send_sem, sems.at[(column * Z + level) * 2 + half], device)

    def arrived(column, level, half, part):
        copy(column, level, half, send_y.at[0], me.mate, part).wait_recv()

    def run(transfer):
        if waiting:
            transfer.wait_send()
        else:
            transfer.start()

    def need(column, level, half, part):
        if not waiting:
            arrived(column, level, half, part)

    def line_sends(level, half, sign, part):
        slot = level * 2 + half
        if sign <= 0:
            pl.when(z < Z - 1)(lambda: run(copy(x, level, half, send_up.at[slot], me.up, upper)))
        if sign >= 0:
            pl.when(z > 0)(lambda: run(copy(x, level, half, send_down.at[slot], me.down, upper)))
        run(copy(x, level, half, send_x.at[slot], me.x_peer, part))
        run(copy(x, level, half, send_y.at[slot], me.y_peer, part))

    def line_step(distance, sign):
        level = z + sign * distance

        def home():
            for half in (core, 1 - core):
                need(x, level, half, upper)
                line_sends(level, half, sign, upper)

        def away():
            need(x, level, 0, upper)
            run(copy(x, level, 0, send_x.at[level * 2], me.x_peer, upper))
            need(x, level, 1, upper)

        valid = (level >= 0) & (level < Z)
        pl.when(valid & me.home)(home)
        pl.when(valid & me.away)(away)

    def first_step():
        @pl.when(me.home)
        def _():
            line_sends(z, core, 0, whole)
            need(x, z, 1 - core, whole)
            line_sends(z, 1 - core, 0, whole)

        @pl.when(me.away)
        def _():
            need(x, z, 0, whole)
            run(copy(x, z, 0, send_x.at[z * 2], me.x_peer, whole))
            need(x, z, 1, whole)

    def peer_step(distance, sign):
        level = z + sign * distance
        part = upper if distance else whole
        valid = (level >= 0) & (level < Z)
        if not waiting:
            @pl.when(valid)
            def _():
                arrived(1 - x, level, 0, part)
                arrived(1 - x, level, 1, part)

        pl.when(valid & me.home)(
            lambda: run(copy(1 - x, level, 1, send_y2.at[level], me.y_peer, part))
        )

    def low_step(distance, sign):
        level = z + sign * distance

        def each(which, carry):
            column, half = which // 2, which % 2
            slot = (column * Z + level) * 2 + half
            if distance:
                need(column, level, half, lower)
            if sign <= 0:
                pl.when(z < Z - 1)(lambda: run(copy(column, level, half, low_up.at[slot], me.up, lower)))
            if sign >= 0:
                pl.when(z > 0)(lambda: run(copy(column, level, half, low_down.at[slot], me.down, lower)))
            return carry

        @pl.when((level >= 0) & (level < Z))
        def _():
            lax.fori_loop(0, 4, each, 0)

    cuts = spans(rows, 608)

    def multiply(pair, half, first, cut):
        width = 2 * block
        depth = pl.ds(pl.multiple_of(pair * width, width), width)
        right = features[depth, pl.ds(pl.multiple_of(half * tokens, tokens), tokens)]
        part = jnp.dot(weight_here[pl.ds(*cut), depth], right, preferred_element_type=jnp.float32)
        where = (half, pl.ds(*cut))
        partial[where] = part if first else partial[where] + part

    def multiply_both(pair, first=False):
        def step(half, carry):
            for cut in cuts:
                multiply(pair, half, first, cut)
            return carry

        lax.fori_loop(0, 2, step, 0)

    waiting = False
    mine = at(x, z, core, whole)
    own_copy = pltpu.make_async_copy(piece, mine, own_sem)
    own_send = remote(piece, mine, own_sem, recv.at[(x * Z + z) * 2 + core], me.mate)
    pl.when(me.home)(own_copy.start)
    pl.when(me.away)(own_send.start)
    pl.when(me.home)(own_copy.wait)
    first_step()
    for sign in (-1, 1):
        line_step(1, sign)
    peer_step(0, 1)
    low_step(0, 0)
    for sign in (-1, 1):
        line_step(2, sign)
    for sign in (-1, 1):
        peer_step(1, sign)
    for sign in (-1, 1):
        low_step(1, sign)
    load_weight.wait()
    multiply_both(x * 2 + z // 2, True)
    for sign in (-1, 1):
        line_step(3, sign)
    for sign in (-1, 1):
        peer_step(2, sign)
    for sign in (-1, 1):
        low_step(2, sign)
    multiply_both((1 - x) * 2 + z // 2)
    for sign in (-1, 1):
        peer_step(3, sign)
    for sign in (-1, 1):
        low_step(3, sign)
    store_features = pltpu.make_async_copy(features, features_out, out_sems.at[0])
    store_features.start()
    near, far = x * 2 + 1 - z // 2, (1 - x) * 2 + 1 - z // 2
    swaps = []
    for at_cut, (start, size) in enumerate(cuts):
        multiply(near, 1 - core, False, (start, size))
        multiply(far, 1 - core, False, (start, size))
        sent = pl.ds(start, -(-size // 8) * 8)
        swaps.append(remote(
            partial.at[1 - core, sent], partial_in.at[sent],
            swap_send.at[at_cut], swap_recv.at[at_cut], me.mate,
        ))
        swaps[-1].start()
    for cut in cuts:
        multiply(near, core, False, cut)
        multiply(far, core, False, cut)

    for load in load_tokens:
        load.wait()

    index = me.pipe * Z + z
    target = labels[...] - index * rows
    peak = jnp.full((1, tokens), -jnp.inf, jnp.float32)
    picked = jnp.zeros((1, tokens), jnp.float32)
    parts = [
        (cut + start, size) for cut, length in cuts for start, size in spans(length, 128)
    ]

    def is_target(start, size):
        return lax.broadcasted_iota(jnp.int32, (size, tokens), 0) + start == target

    for start, size in parts:
        for swap, cut in zip(swaps, cuts):
            if start == cut[0]:
                swap.wait_recv()
        where = pl.ds(start, size)
        logits = partial[core, where] + partial_in[where]
        partial_in[where] = logits
        peak = jnp.maximum(peak, jnp.max(logits, axis=0, keepdims=True))
        picked += jnp.sum(jnp.where(is_target(start, size), logits, 0.0), axis=0, keepdims=True)
    total = jnp.zeros((1, tokens), jnp.float32)
    for start, size in parts:
        total += jnp.sum(jnp.exp(partial_in[pl.ds(start, size)] - peak), axis=0, keepdims=True)
    stats[index] = jnp.concatenate([peak, total, picked, jnp.zeros((5, tokens), jnp.float32)], axis=0)

    def stat_copy(step):
        other = (index + step) % n
        device = {"pipe": other // Z, "tensor": other % Z}
        return remote(stats.at[index], stats.at[index], stat_send.at[step], stat_recv.at[index], device)

    def send_stat(step, carry):
        stat_copy(step).start()
        return carry

    def wait_stat(step, carry):
        other = (index + step) % n
        remote(
            stats.at[other], stats.at[other], stat_send.at[step], stat_recv.at[other], me.mate
        ).wait_recv()
        return carry

    def wait_stat_send(step, carry):
        stat_copy(step).wait_send()
        return carry

    lax.fori_loop(1, n, send_stat, 0)
    waiting = True
    pl.when(me.away)(own_send.wait_send)
    first_step()
    peer_step(0, 1)
    low_step(0, 0)
    for distance in (1, 2, 3):
        for sign in (-1, 1):
            line_step(distance, sign)
            peer_step(distance, sign)
            low_step(distance, sign)

    lax.fori_loop(1, n, wait_stat, 0)
    every = stats[...]
    peaks, totals, picks = every[:, 0], every[:, 1], every[:, 2]
    row_peak = jnp.max(peaks, axis=0, keepdims=True)
    row_total = jnp.sum(totals * jnp.exp(peaks - row_peak), axis=0, keepdims=True)
    loss_out[...] = row_peak + jnp.log(row_total) - jnp.sum(picks, axis=0, keepdims=True)
    scale = loss_weight[...]
    inverse = 1.0 / row_total
    for start, size in parts:
        where = pl.ds(start, size)
        share = jnp.exp(partial_in[where] - row_peak) * inverse
        hit = jnp.where(is_target(start, size), 1.0, 0.0)
        grads[core, where] = (scale * (share - hit)).astype(jnp.bfloat16)
    share_grad = remote(grads.at[core], grads.at[core], mate_sems.at[0], mate_sems.at[1], me.mate)
    share_grad.start()

    def keep(half, sem):
        there = grad_out.at[:, pl.ds(pl.multiple_of(half * tokens, tokens), tokens)]
        return pltpu.make_async_copy(grads.at[half], there, sem)

    keep(core, out_sems.at[1]).start()

    def multiply_back(pair, half):
        width = 2 * block
        depth = pl.ds(pl.multiple_of(pair * width, width), width)
        term[depth, pl.ds(pl.multiple_of(half * tokens, tokens), tokens)] = lax.dot_general(
            weight_here[:, depth], grads[half], (((0,), (0,)), ((), ())), preferred_element_type=jnp.float32
        ).astype(jnp.bfloat16)

    def back(step, carry):
        multiply_back(jnp.where(step % 2 == 0, far, near), jnp.where(step < 2, core, 1 - core))
        return carry

    def back_rest(step, carry):
        column = jnp.where(step % 2 == 0, 1 - x, x)
        multiply_back(column * 2 + z // 2, step // 2)
        return carry

    lax.fori_loop(0, 2, back, 0)
    share_grad.wait_recv()
    keep(1 - core, out_sems.at[2]).start()
    lax.fori_loop(2, 4, back, 0)
    reduce_rows(me, block, term, hidden_out, lambda: lax.fori_loop(0, 4, back_rest, 0), *reduce_scratch)

    lax.fori_loop(1, n, wait_stat_send, 0)
    for swap in swaps:
        swap.wait_send()
    share_grad.wait_send()
    keep(core, out_sems.at[1]).wait()
    keep(1 - core, out_sems.at[2]).wait()
    store_features.wait()


def head(hidden_t, head_weight, labels, loss_weight, n):
    block, tokens = hidden_t.shape
    rows, width = head_weight.shape
    padded = -(-rows // 8) * 8
    low = block // 100 * 16
    dma = pltpu.SemaphoreType.DMA

    def pieces(count):
        return pltpu.VMEM((count, block, tokens), jnp.bfloat16)

    one = pltpu.VMEM((block, tokens), jnp.bfloat16)
    return pl.pallas_call(
        functools.partial(head_kernel, n, block),
        out_shape=(
            jax.ShapeDtypeStruct((width, 2 * tokens), jnp.bfloat16),
            jax.ShapeDtypeStruct((rows, 2 * tokens), jnp.bfloat16),
            jax.ShapeDtypeStruct((1, tokens), jnp.float32),
            jax.ShapeDtypeStruct((block, tokens), jnp.bfloat16),
        ),
        in_specs=[HBM, ANY, HBM, HBM],
        out_specs=(ANY, ANY, VMEM, VMEM),
        scratch_shapes=[
            pltpu.VMEM((width, 2 * tokens), jnp.bfloat16),
            pltpu.VMEM((rows, width), jnp.bfloat16),
            pltpu.VMEM((2, padded, tokens), jnp.float32),
            pltpu.VMEM((padded, tokens), jnp.float32),
            pltpu.VMEM((2, rows, tokens), jnp.bfloat16),
            pltpu.VMEM((width, 2 * tokens), jnp.bfloat16),
            pltpu.VMEM((n, 8, tokens), jnp.float32),
            pltpu.VMEM((1, tokens), jnp.int32),
            pltpu.VMEM((1, tokens), jnp.float32),
            dma((16,)), dma((16,)), dma((8,)), dma((8,)), dma((16,)), dma((16,)), dma((8,)), dma((8,)), dma((4,)),
            dma, dma, dma((2,)), dma((2,)), dma((2,)), dma((n,)), dma((n,)), dma((3,)), dma((2,)),
            pieces(12), pieces(8), pieces(8), pieces(8), pieces(4), pieces(8), one, one,
            pltpu.VMEM((16, low, tokens), jnp.bfloat16), pieces(4),
            dma((12,)), dma((8,)), dma((8,)), dma((8,)), dma, dma((16,)), dma((16,)),
            dma((4,)), dma((4,)), dma((12,)), dma((8,)), dma,
        ],
        compiler_params=pltpu.CompilerParams(
            collective_id=0, has_side_effects=True, vmem_limit_bytes=VMEM_BYTES
        ),
    )(hidden_t, head_weight, labels, loss_weight)


def reduce_rows(
    me, block, term, out, finish_term,
    from_y, from_x, from_below, from_above, passed, summed, final, landed, from_low, at_home,
    recv_y, recv_x, recv_below, recv_above, recv_final, recv_low, send_low,
    send_x, send_pass, send_y, send_z, send_final,
):
    tokens = out.shape[1]
    x, z, core = me.x, me.z, me.core

    low = from_low.shape[1]
    whole, upper, lower = (0, block), (low, block - low), (0, low)

    top = z // 2
    order = (3 * (1 - top), 2 - top, 1 - z + 4 * top, z)
    last = Z - 1

    def own(column, level, half, part):
        start = pl.multiple_of((column * Z + level) * block + part[0], 16)
        return term.at[pl.ds(start, part[1]), pl.ds(pl.multiple_of(half * tokens, tokens), tokens)]

    def cut(ref, turn, slot):
        start, size = whole if turn == last else upper
        return ref.at[slot, pl.ds(start, size)]

    def mine(peer, turn, half):
        if turn == last:
            return at_home.at[peer * 2 + half]
        return own(1 - x if peer else x, order[turn], half, upper)

    def away_cross(turn):
        level = order[turn]
        slot = level * 2
        return remote(mine(1, turn, 0), cut(from_x, turn, slot), send_x.at[level], recv_x.at[slot], me.x_peer)

    def away_diagonal(turn):
        slot = 8 + order[turn]
        return remote(mine(1, turn, 1), cut(from_y, turn, slot), send_y.at[slot], recv_y.at[slot], me.y_peer)

    def away_line(turn, half):
        slot = order[turn] * 2 + half
        source = mine(0, turn, 1) if half else cut(passed, turn, order[turn])
        return remote(source, cut(from_y, turn, slot), send_y.at[slot], recv_y.at[slot], me.y_peer)

    def home_cross(turn, half):
        level = order[turn]
        slot = level * 2 + half
        source = cut(passed, turn, level) if half else mine(1, turn, 0)
        sem = send_pass.at[level] if half else send_x.at[level]
        return remote(source, cut(from_x, turn, slot), sem, recv_x.at[slot], me.x_peer)

    def rise(level, half):
        slot = level * 2 + half
        return remote(cut(summed, 0, slot), cut(from_below, 0, slot), send_z.at[slot], recv_below.at[slot], me.up)

    def sink(level, half):
        slot = level * 2 + half
        return remote(cut(summed, 0, slot), cut(from_above, 0, slot), send_z.at[slot], recv_above.at[slot], me.down)

    def low_copy(turn, which):
        level = order[turn]
        source = own(x + which // 2 * (1 - 2 * x), level, which % 2, lower)
        slot, there = z * 4 + which, level * 4 + which
        return remote(source, from_low.at[slot], send_low.at[there], recv_low.at[slot], {"tensor": level})

    def each_low(act):
        def step(which, carry):
            act(which)
            return carry

        lax.fori_loop(0, 4, step, 0)

    def settle(which):
        column, half = x + which // 2 * (1 - 2 * x), which % 2
        total = f32(own(column, z, half, lower))
        for step in range(1, Z):
            slot = (z + step) % Z * 4 + which
            here = from_low.at[slot]
            remote(here, here, send_final, recv_low.at[slot], me.mate).wait_recv()
            total += f32(here)
        at_home[which, pl.ds(0, low)] = total.astype(jnp.bfloat16)
        at_home[which, pl.ds(low, block - low)] = own(column, z, half, upper)[...]

    def hand_over():
        return remote(final, landed, send_final, recv_final, me.mate)

    def f32(ref):
        return ref[...].astype(jnp.float32)

    for turn in (0, 1):
        each_low(lambda which: low_copy(turn, which).start())

    @pl.when(me.away)
    def _():
        for turn in (0, 1):
            away_cross(turn).start()
            away_diagonal(turn).start()
            away_line(turn, 1).start()

    @pl.when(me.home)
    def _():
        for turn in (0, 1):
            home_cross(turn, 0).start()

    finish_term()
    each_low(lambda which: low_copy(2, which).start())

    def away_turn(turn):
        level = order[turn]
        away_cross(turn).wait_recv()
        cut(passed, turn, level)[...] = (
            f32(mine(0, turn, 0)) + f32(cut(from_x, turn, level * 2))
        ).astype(jnp.bfloat16)
        away_line(turn, 0).start()
        if turn + 2 < Z:
            away_cross(turn + 2).start()
            away_diagonal(turn + 2).start()
            away_line(turn + 2, 1).start()

    def pass_on(turn):
        level = order[turn]
        away_diagonal(turn).wait_recv()
        cut(passed, turn, level)[...] = (
            f32(mine(1, turn, 1)) + f32(cut(from_y, turn, 8 + level))
        ).astype(jnp.bfloat16)
        home_cross(turn, 1).start()

    def gather(turn, half):
        slot = order[turn] * 2 + half
        total = f32(mine(0, turn, half))
        for inbox, sems in ((from_y, recv_y), (from_x, recv_x)):
            here = cut(inbox, turn, slot)
            remote(here, here, send_final, sems.at[slot], me.mate).wait_recv()
            total += f32(here)
        return total

    def send_on(turn):
        level = order[turn]
        for half in (1, 0):
            slot = level * 2 + half
            total = gather(turn, half)
            kept = cut(summed, turn, slot)
            kept[...] = total.astype(jnp.bfloat16)

            @pl.when((level < z) & (z < Z - 1))
            def _():
                sink(level, half).wait_recv()
                kept[...] = (total + f32(cut(from_above, turn, slot))).astype(jnp.bfloat16)

            @pl.when((level > z) & (z > 0))
            def _():
                rise(level, half).wait_recv()
                kept[...] = (total + f32(cut(from_below, turn, slot))).astype(jnp.bfloat16)

            pl.when(level < z)(lambda: sink(level, half).start())
            pl.when(level > z)(lambda: rise(level, half).start())

    def finish(half, ref):
        slot = z * 2 + half
        total = gather(last, half)
        ref[pl.ds(0, low)] = total[:low].astype(jnp.bfloat16)
        rest, there = total[low:], pl.ds(low, block - low)
        above, below = cut(from_above, 0, slot), cut(from_below, 0, slot)

        @pl.when(z == 0)
        def _():
            sink(z, half).wait_recv()
            ref[there] = (rest + f32(above)).astype(jnp.bfloat16)

        @pl.when(z == Z - 1)
        def _():
            rise(z, half).wait_recv()
            ref[there] = (rest + f32(below)).astype(jnp.bfloat16)

        @pl.when((z > 0) & (z < Z - 1))
        def _():
            sink(z, half).wait_recv()
            rise(z, half).wait_recv()
            ref[there] = (rest + f32(above) + f32(below)).astype(jnp.bfloat16)

    pl.when(me.away)(lambda: away_turn(0))

    @pl.when(me.home)
    def _():
        pass_on(0)
        home_cross(2, 0).start()
        pass_on(1)

    each_low(settle)

    @pl.when(me.away)
    def _():
        for turn in (1, 2, 3):
            away_turn(turn)
        for turn in range(Z):
            away_cross(turn).wait_send()
            away_diagonal(turn).wait_send()
            away_line(turn, 1).wait_send()
            away_line(turn, 0).wait_send()
        hand_over().wait_recv()
        out[...] = landed[...]

    @pl.when(me.home)
    def _():
        send_on(0)
        home_cross(3, 0).start()
        pass_on(2)
        send_on(1)
        pass_on(3)
        send_on(2)
        finish(1 - core, final)
        hand_over().start()
        finish(core, out)
        for turn in range(Z):
            level = order[turn]
            for half in (0, 1):
                home_cross(turn, half).wait_send()
                if turn < last:
                    pl.when(level < z)(lambda: sink(level, half).wait_send())
                    pl.when(level > z)(lambda: rise(level, half).wait_send())
        hand_over().wait_send()

    for turn in range(last):
        each_low(lambda which: low_copy(turn, which).wait_send())


def per_device_chips(n, hidden, head_weight, labels, loss_weight):
    tokens, block = hidden.shape
    features, logit_grad, token_loss, hidden_grad = head(
        hidden.T, head_weight, labels.reshape(1, tokens), loss_weight.reshape(1, tokens), n
    )
    head_grad = lax.dot_general(
        logit_grad, features, (((1,), (1,)), ((), ())), preferred_element_type=jnp.float32
    ).astype(jnp.bfloat16)
    return hidden_grad.T, head_grad, token_loss.reshape(tokens)


def per_device(hidden, head_weight, labels, loss_weight):
    tokens = hidden.shape[0]
    rows = head_weight.shape[0]
    features = lax.all_gather(hidden, GROUP, axis=1, tiled=True)
    features = lax.all_to_all(features, "dp", split_axis=1, concat_axis=0, tiled=True)
    partial = lax.dot_general(
        head_weight, features, (((1,), (1,)), ((), ())), preferred_element_type=jnp.float32
    )
    logits = lax.psum_scatter(partial, "dp", scatter_dimension=1, tiled=True)
    entries = lax.axis_index(GROUP) * rows + jnp.arange(rows, dtype=jnp.int32)
    mask = (entries[:, None] == labels[None, :]).astype(jnp.float32)
    row_peak = lax.pmax(jnp.max(logits, axis=0), GROUP)
    shifted_exp = jnp.exp(logits - row_peak[None, :])
    row_total, picked = lax.psum((jnp.sum(shifted_exp, axis=0), jnp.sum(mask * logits, axis=0)), GROUP)
    token_loss = row_peak + jnp.log(row_total) - picked
    grad = (loss_weight[None, :] * (shifted_exp / row_total[None, :] - mask)).astype(jnp.bfloat16)
    grad = lax.all_gather(grad, "dp", axis=1, tiled=True)
    head_grad = jnp.dot(grad, features, preferred_element_type=jnp.float32).astype(jnp.bfloat16)
    term = lax.dot_general(grad, head_weight, (((0,), (0,)), ((), ())), preferred_element_type=jnp.float32)
    term = lax.all_to_all(term, "dp", split_axis=0, concat_axis=1, tiled=True)
    hidden_grad = lax.psum_scatter(term, GROUP, scatter_dimension=1, tiled=True).astype(jnp.bfloat16)
    return hidden_grad, head_grad, token_loss


def solution(mesh):
    sizes = dict(mesh.shape)
    if (sizes["pipe"], sizes["tensor"], sizes["dp"]) == (4, Z, 2):
        body = functools.partial(per_device_chips, 4 * Z)
    else:
        body = per_device
    return jax.shard_map(
        body,
        mesh=mesh,
        in_specs=(P("dp", GROUP), P(GROUP, "dp"), P("dp"), P("dp")),
        out_specs=(P("dp", GROUP), P(GROUP, "dp"), P("dp")),
        check_vma=False,
    )
```
